128 devices in a mesh: feat: 4 (over x), node: 32 (over z, y, core).
Axes of the slice: x: 4, y: 4, z: 4, core: 2. Of those that a mesh axis runs over, the one named last changes fastest.
Arguments:
- features: bfloat16 [65536, 2048], P('node', 'feat'), may hold values from -6 to 6
- self_w1: bfloat16 [2048, 1024], P('feat'), may hold values from -0.125 to 0.125
- neigh_w1: bfloat16 [2048, 1024], P('feat'), may hold values from -0.125 to 0.125
- self_w2: bfloat16 [1024, 1024], P('feat'), may hold values from -0.1875 to 0.1875
- neigh_w2: bfloat16 [1024, 1024], P('feat'), may hold values from -0.1875 to 0.1875
- source_tiles1: int32 [1024], P('node'), may hold values from 0 to 15
- owner_blocks1: int32 [1024, 1], P('node'), may hold values from 0 to 31; in each aligned block of 32 rows (0 to 31, 32 to 63, ...) at most 2 rows name the same one
- target_tiles1: int32 [1024], P('node'), may hold values from 0 to 15
- tile_masks1: int32 [1024, 128, 128], P('node'), may hold values 0 or 1
- source_tiles2: int32 [1024], P('node'), may hold values from 0 to 15
- owner_blocks2: int32 [1024, 1], P('node'), may hold values from 0 to 31; in each aligned block of 32 rows (0 to 31, 32 to 63, ...) at most 2 rows name the same one
- target_tiles2: int32 [1024], P('node'), may hold values from 0 to 15
- tile_masks2: int32 [1024, 128, 128], P('node'), may hold values 0 or 1
- cotangent: bfloat16 [65536, 1024], P('node', 'feat'), may hold values from -0.0234375 to 0.0234375
Outputs:
- hidden2: bfloat16 [65536, 1024], P('node', 'feat')
- grad_self2: float32 [1024, 1024], P(('feat', 'node'))
- grad_neigh2: float32 [1024, 1024], P(('feat', 'node'))
The draws below stay inside these ranges and needn't reach their ends.
Inputs may be any that keep to these rules, and one draw needn't show every extreme that they name: `owner_blocks1`: among the 32 entries of one node block, at most 2 name the same written block. `owner_blocks2`: among the 32 entries of one node block, at most 2 name the same written block.
All inputs are finite; a program needn't handle non-finite values. No bound on the sum of `tile_masks1` or of `tile_masks2` on one device may be relied on, other than what follows from the above.
Results may differ from the reference program's by a relative error of at most 0.0061.
Values may be sent and summed in bfloat16 or wider, within the bound.
A program may use at most 128 MiB of HBM per device.

```python
import math
import jax
import jax.numpy as jnp
import numpy as np
from jax import lax

F = 2048
H = 1024
TILE = 128
TILES_DEV = 16
E_DEV = 32
CAP = 2
NODES = 65536
TILE_LIST = 1024
N_NODE = 32


def set_ends(values, rng, least, top_value):
    longest = values.shape.index(max(values.shape))
    spots = []
    for shift in (0, 1):
        where = [jax.random.randint(jax.random.fold_in(rng, axis), (), 0, length) for axis, length in enumerate(values.shape)]
        where[longest] = (where[longest] + shift) % values.shape[longest]
        spots.append(tuple(where))
    return values.at[spots[0]].set(least).at[spots[1]].set(top_value)


def level_of(stream_key, dims, cuts, low, largest):
    loudness, own = 1.0, jax.random.fold_in(stream_key, 6)
    for axis_at, blocks in cuts:
        draws = jnp.exp(jax.random.uniform(jax.random.fold_in(own, axis_at), (blocks,), jnp.float32, low / len(cuts), largest / len(cuts)))
        loudness = loudness * jnp.repeat(draws, dims[axis_at] // blocks).reshape([-1 if axis == axis_at else 1 for axis in range(len(dims))])
    return loudness


def shared_out(rng, own, number, rows, amount, top, most, lean):
    ranking = jax.random.permutation(rng, amount)
    packed, common = shares(amount, rows * top, most, lean, True), shares(amount, rows * top, most, lean, False)
    places = jnp.arange(amount)

    def named(sizes, offset_by):
        used = int((sizes > 0).sum())
        fixed = max(1, used // 4)
        passed = fixed + (places - fixed + offset_by * (used - fixed)) % max(1, amount - fixed)
        return jnp.zeros((amount,), jnp.int32).at[ranking[jnp.where(places < fixed, places, passed)]].set(jnp.asarray(sizes, jnp.int32))

    sizes = jnp.where(number % 4 == 0, named(packed, number // 4), named(common, number - number // 4 - 1))
    mixed = jax.random.permutation(jax.random.fold_in(own, 3), amount)
    source_of, receiver = mixed[0:amount // 2 * 2:2], mixed[1:amount // 2 * 2:2]
    room = jnp.minimum(sizes[source_of] - 1, most - sizes[receiver]) // 2
    room = jnp.where((source_of == ranking[0]) | (receiver == ranking[0]) | (sizes[receiver] == 0), 0, jnp.maximum(room, 0))
    passed = jax.random.randint(jax.random.fold_in(own, 4), (amount // 2,), 0, 1 << 20) % (room + 1)
    sizes = sizes.at[source_of].add(-passed).at[receiver].add(passed)
    items = jnp.searchsorted(jnp.cumsum(sizes), jnp.arange(rows * top), side="right").astype(jnp.int32)
    grid = items.reshape(top, rows).T
    grid = grid[jax.random.permutation(jax.random.fold_in(own, 1), rows)]
    offset_by = jax.random.randint(jax.random.fold_in(own, 2), (rows, 1), 0, top)
    return jnp.take_along_axis(grid, (jnp.arange(top)[None, :] + offset_by) % top, axis=1)


def shares(number_of, total, most, lean, full):
    portions = [(1 << 20) // math.isqrt(standing ** lean) + 1 for standing in range(1, number_of + 1)]
    largest = most if full else min(most, max(-(-total // number_of), total * portions[0] // sum(portions)))
    least = 1 if total - largest >= number_of - 1 else 0
    given, rest = [largest] + [least] * (number_of - 1), total - largest - least * (number_of - 1)
    while rest > 0:
        free = [i for i in range(1, number_of) if given[i] < largest] or [i for i in range(1, number_of) if given[i] < most]
        whole, remaining = sum([portions[i] for i in free]), rest
        for i in free:
            addition = min(most - given[i], max(1, remaining * portions[i] // whole), rest)
            given[i] = given[i] + addition
            rest = rest - addition
    return np.array(given)


def scatter_about(rng, extent, deviation, limit, cuts=(), kind=jnp.bfloat16):
    loudness = level_of(rng, extent, cuts, -0.22, 0.18) if cuts else 1.0
    array = jax.random.normal(rng, extent, jnp.float32) * deviation * loudness
    return jnp.minimum(jnp.maximum(array, -limit), limit).astype(kind)


def setup_inputs(seed: int = 0) -> dict:
    streams_of = jax.random.split(jax.random.key(seed), 15)
    features = scatter_about(streams_of[0], (NODES, F), 1.0, 6.0, ((0, 32), (1, 4)))
    self_w1 = scatter_about(streams_of[1], (F, H), F ** -0.5, 0.125, ((0, 4),))
    neigh_w1 = scatter_about(streams_of[2], (F, H), F ** -0.5, 0.125, ((0, 4),))
    self_w2 = scatter_about(streams_of[3], (H, H), H ** -0.5, 0.1875, ((0, 4),))
    neigh_w2 = scatter_about(streams_of[4], (H, H), H ** -0.5, 0.1875, ((0, 4),))
    source_tiles1 = set_ends(jax.random.randint(streams_of[5], (TILE_LIST,), 0, TILES_DEV), jax.random.fold_in(streams_of[5], 1), 0, TILES_DEV - 1).astype(jnp.int32)
    owner_blocks1_keys = jax.random.split(jax.random.fold_in(streams_of[6], 1), TILE_LIST // E_DEV)
    owner_blocks1_turns = jax.random.permutation(jax.random.fold_in(streams_of[6], 3), TILE_LIST // E_DEV)
    owner_blocks1 = jax.vmap(lambda own, number: shared_out(jax.random.fold_in(streams_of[6], 2), own, number, E_DEV, N_NODE, 1, CAP, 2))(owner_blocks1_keys, owner_blocks1_turns).reshape((TILE_LIST, 1))
    target_tiles1 = set_ends(jax.random.randint(streams_of[7], (TILE_LIST,), 0, TILES_DEV), jax.random.fold_in(streams_of[7], 1), 0, TILES_DEV - 1).astype(jnp.int32)
    tile_masks1 = set_ends((jax.random.randint(streams_of[8], (TILE_LIST, TILE, TILE), 0, 16) < 1).astype(jnp.int32), jax.random.fold_in(streams_of[8], 1), 0, 1)
    source_tiles2 = set_ends(jax.random.randint(streams_of[9], (TILE_LIST,), 0, TILES_DEV), jax.random.fold_in(streams_of[9], 1), 0, TILES_DEV - 1).astype(jnp.int32)
    owner_blocks2_keys = jax.random.split(jax.random.fold_in(streams_of[10], 1), TILE_LIST // E_DEV)
    owner_blocks2_turns = jax.random.permutation(jax.random.fold_in(streams_of[10], 3), TILE_LIST // E_DEV)
    owner_blocks2 = jax.vmap(lambda own, number: shared_out(jax.random.fold_in(streams_of[10], 2), own, number, E_DEV, N_NODE, 1, CAP, 2))(owner_blocks2_keys, owner_blocks2_turns).reshape((TILE_LIST, 1))
    target_tiles2 = set_ends(jax.random.randint(streams_of[11], (TILE_LIST,), 0, TILES_DEV), jax.random.fold_in(streams_of[11], 1), 0, TILES_DEV - 1).astype(jnp.int32)
    tile_masks2 = set_ends((jax.random.randint(streams_of[12], (TILE_LIST, TILE, TILE), 0, 16) < 1).astype(jnp.int32), jax.random.fold_in(streams_of[12], 1), 0, 1)
    cotangent = scatter_about(streams_of[13], (NODES, H), NODES ** -0.5, 0.0234375, ((0, 32), (1, 4)))
    return {"features": features, "self_w1": self_w1, "neigh_w1": neigh_w1, "self_w2": self_w2, "neigh_w2": neigh_w2, "source_tiles1": source_tiles1, "owner_blocks1": owner_blocks1, "target_tiles1": target_tiles1, "tile_masks1": tile_masks1, "source_tiles2": source_tiles2, "owner_blocks2": owner_blocks2, "target_tiles2": target_tiles2, "tile_masks2": tile_masks2, "cotangent": cotangent}


def aggregate(values, source_tiles, owner_blocks, target_tiles, tile_masks):
    node_count, feature_width = values.shape
    tile_count = node_count // TILE
    blocks = values.reshape(tile_count, TILE, feature_width)
    targets = owner_blocks[:, 0] * TILES_DEV + target_tiles

    def visit(totals, source):
        begin = source * E_DEV
        masks_here = lax.dynamic_slice_in_dim(tile_masks, begin, E_DEV, 0).astype(jnp.float32)
        read_tiles = source * TILES_DEV + lax.dynamic_slice_in_dim(source_tiles, begin, E_DEV, 0)
        picked = blocks[read_tiles].astype(jnp.float32)
        pieces = jnp.einsum("eac,eaw->ecw", masks_here, picked).astype(jnp.bfloat16)
        pieces = lax.optimization_barrier(pieces)
        written = lax.dynamic_slice_in_dim(targets, begin, E_DEV, 0)
        summed = totals[0].at[written].add(pieces.astype(jnp.float32))
        degree = totals[1].at[written].add(jnp.sum(masks_here, axis=1))
        return (summed, degree), None

    initial = (jnp.zeros((tile_count, TILE, feature_width), jnp.float32), jnp.zeros((tile_count, TILE), jnp.float32))
    finals, ignored = lax.scan(visit, initial, jnp.arange(N_NODE, dtype=jnp.int32))
    summed, degree = finals
    return (summed / jnp.maximum(degree, 1.0)[:, :, None]).reshape(node_count, feature_width)


def reference(features, self_w1, neigh_w1, self_w2, neigh_w2, source_tiles1, owner_blocks1, target_tiles1, tile_masks1, source_tiles2, owner_blocks2, target_tiles2, tile_masks2, cotangent):
    self1 = jnp.dot(features, self_w1, preferred_element_type=jnp.float32)
    proj1 = jnp.dot(features, neigh_w1, preferred_element_type=jnp.float32).astype(jnp.bfloat16)
    mean1 = aggregate(proj1, source_tiles1, owner_blocks1, target_tiles1, tile_masks1)
    hidden1 = jax.nn.relu(self1 + mean1).astype(jnp.bfloat16)
    mean2 = aggregate(hidden1, source_tiles2, owner_blocks2, target_tiles2, tile_masks2).astype(jnp.bfloat16)
    pre2 = jnp.dot(hidden1, self_w2, preferred_element_type=jnp.float32) + jnp.dot(mean2, neigh_w2, preferred_element_type=jnp.float32)
    sigma = jax.nn.sigmoid(pre2)
    hidden2 = (pre2 * sigma).astype(jnp.bfloat16)
    slope = (cotangent.astype(jnp.float32) * sigma * (1.0 + pre2 * (1.0 - sigma))).astype(jnp.bfloat16)
    grad_self2 = jnp.dot(hidden1.T, slope, preferred_element_type=jnp.float32)
    grad_neigh2 = jnp.dot(mean2.T, slope, preferred_element_type=jnp.float32)
    return (hidden2, grad_self2, grad_neigh2)
```

```python
import functools

import jax
import jax.numpy as jnp
from jax import lax
from jax.experimental import pallas as pl
from jax.experimental.pallas import tpu as pltpu
from jax.sharding import PartitionSpec as P

MESH = pl.DeviceIdType.MESH
BF = jnp.bfloat16
F32 = jnp.float32
NEIGH, SELF = 0, 1


def dot(a, b):
    return jnp.dot(a, b, preferred_element_type=F32)


def kernel(
    feat_hbm, ws1_hbm, wn1_hbm, ws2_hbm, wn2_hbm,
    src1, own1, tgt1, mask1_hbm, src2, own2, tgt2, mask2_hbm, cot_hbm,
    hid2_out, gs_out, gn_out,
    feat, w1n, w1s, mask1, mask2, maskt, cnt, tab,
    p0, p1, p2, p3, own, a0, a1, a2, a3, b0, b1, b2, b3, proj0, proj1, hid0, hid1,
    msg_out, msg_in, vcol, ccol, lhs, rdeg,
    send0, send1, recv0, recv1, recv2, recv3, h0, h1, m0, m1, xoth0, xoth1, xt,
    cot, w2, slope_own, slope_oth,
    g0, g1, r1a, r1b, s1a, s1b, r2a, r2b, s2a, s2b, r3a, r3b, fin, finr,
    ld, meta_s, meta_r, ra_s, ra_r, rb_s, rb_r, aa_s, aa_r, rows_s, rows_r,
    cot_s, cot_r, w2_s, w2_r, wd_s, wd_r, x_s, x_r, sl_s, sl_r, h2_s, h2_r,
    g1_s, g1_r, g2_s, g2_r, g3_s, g3_r, fn_s, fn_r,
):
    f = lax.axis_index("feat")
    n = lax.axis_index("node")
    z, y, core = n // 8, (n // 2) % 4, n % 2
    sign = 1 - 2 * core
    right, left, opp = (f + 1) % 4, (f + 3) % 4, (f + 2) % 4
    other = n + sign
    proj, hid = (proj0, proj1), (hid0, hid1)
    psend, buf_a, buf_b = (p0, p1, p2, p3), (a0, a1, a2, a3), (b0, b1, b2, b3)
    sendbuf, recv = (send0, send1), (recv0, recv1, recv2, recv3)
    hm, xoth = ((h0, h1), (m0, m1)), (xoth0, xoth1)
    r1, s1, r2, s2, r3 = (r1a, r1b), (s1a, s1b), (r2a, r2b), (s2a, s2b), (r3a, r3b)

    def peer(i):
        j, ii, dc = i // 8, (i // 2) % 4, i % 2
        zz = (z + sign * ii + 4) % 4
        yy = (y + sign * ((ii + j) % 4) + 4) % 4
        return (f, zz * 8 + yy * 2 + (core + dc) % 2)

    def remote(src, dst, ss, rs, dev):
        return pltpu.make_async_remote_copy(
            src_ref=src, dst_ref=dst, send_sem=ss, recv_sem=rs, device_id=dev, device_id_type=MESH
        )

    def local(src, dst, k):
        return pltpu.make_async_copy(src, dst, ld.at[k])

    loads = [
        local(feat_hbm, feat, 0),
        local(wn1_hbm, w1n, 1),
        local(ws1_hbm, w1s, 2),
        local(mask1_hbm, mask1, 3),
        local(cot_hbm.at[pl.ds(pl.multiple_of(f * 512, 512), 512)], cot.at[f], 4),
    ]
    for m, ref in ((0, ws2_hbm), (1, wn2_hbm)):
        for c in range(2):
            loads.append(local(ref.at[pl.ds(c * 128, 128)], w2.at[m, f, c], 5 + 2 * m + c))
    load_mask2 = local(mask2_hbm, mask2, 9)
    for c in [*loads, load_mask2]:
        c.start()

    barrier = pltpu.get_barrier_semaphore()

    @pl.loop(1, 32)
    def _(i):
        pl.semaphore_signal(barrier, inc=1, device_id=peer(i), device_id_type=MESH)

    for d in (right, left, opp):
        pl.semaphore_signal(barrier, inc=1, device_id=(d, n), device_id_type=MESH)
    pl.semaphore_wait(barrier, 34)

    def project(mat, j, where):
        cols = pl.ds(pl.multiple_of(j * 256, 256), 256)

        @pl.loop(0, 4)
        def _(t):
            rows = pl.ds(pl.multiple_of(t * 512, 512), 512)
            part = dot(feat[rows, :], (w1n, w1s)[mat][:, cols])
            for c in range(2):
                half = part[:, c * 128 : (c + 1) * 128]
                if where is None:
                    own[2 * mat + c, pl.ds(t * 4, 4)] = half.reshape(4, 128, 128)
                else:
                    psend[2 * mat + c][where, rows, :] = half.astype(BF)

    lo, hi = pl.ds(0, 1024), pl.ds(1024, 1024)

    def copies_a(q):
        return [
            remote(psend[q].at[0, lo], buf_a[q].at[0], ra_s.at[q, 0], ra_r.at[q, 0], (right, n)),
            remote(psend[q].at[0, hi], buf_a[q].at[1], ra_s.at[q, 1], ra_r.at[q, 1], (left, n)),
        ]

    def copies_direct(q):
        return [
            remote(psend[q].at[1, hi], buf_b[q].at[0, hi], rb_s.at[q, 0], rb_r.at[q, 0], (right, n)),
            remote(psend[q].at[2, lo], buf_b[q].at[1, lo], rb_s.at[q, 1], rb_r.at[q, 1], (left, n)),
        ]

    def copies_added(q):
        return [
            remote(psend[q].at[1, lo], buf_b[q].at[0, lo], rb_s.at[q, 2], rb_r.at[q, 2], (right, n)),
            remote(psend[q].at[2, hi], buf_b[q].at[1, hi], rb_s.at[q, 3], rb_r.at[q, 3], (left, n)),
        ]

    def start(copies):
        for c in copies:
            c.start()

    def ring_start(q):
        start(copies_a(q))
        start(copies_direct(q))

    def ring_add(q):
        a, b = copies_a(q), copies_added(q)
        for s, base in ((0, 0), (1, 1024)):
            a[s].wait_recv()

            @pl.loop(0, 4)
            def _(t):
                rows = pl.ds(pl.multiple_of(t * 256 + base, 256), 256)
                from_rows = pl.ds(pl.multiple_of(t * 256, 256), 256)
                total = psend[q][1 + s, rows, :].astype(F32) + buf_a[q][s, from_rows, :].astype(F32)
                psend[q][1 + s, rows, :] = total.astype(BF)

            b[s].start()

    def ring_end(q):
        for c in copies_direct(q) + copies_added(q):
            c.wait_recv()

        @pl.loop(0, 8)
        def _(t):
            rows = pl.ds(pl.multiple_of(t * 256, 256), 256)
            got = buf_b[q][0, rows, :].astype(F32) + buf_b[q][1, rows, :].astype(F32)
            total = own[q, pl.ds(t * 2, 2)] + got.reshape(2, 128, 128)
            if q < 2:
                proj[q][pl.ds(t * 2, 2)] = total.astype(BF)
            else:
                own[q, pl.ds(t * 2, 2)] = total

    def masks_of(layer, mask):
        @pl.loop(0, 32)
        def _(e):
            m = mask[e].astype(F32)
            cnt[layer, e] = jnp.broadcast_to(jnp.sum(m, axis=0, keepdims=True), (8, 128))
            maskt[layer, e] = m.T.astype(BF)

    def slots_of(layer, owners, sources):
        @pl.loop(0, 32)
        def _(i):
            who = peer(i)[1]

            def look(e, carry):
                seen, first, second = carry
                hit = owners[e, 0] == who
                first = jnp.where(jnp.logical_and(hit, seen == 0), e, first)
                second = jnp.where(jnp.logical_and(hit, seen == 1), e, second)
                return seen + hit.astype(jnp.int32), first, second

            zero = jnp.int32(0)
            seen, first, second = lax.fori_loop(0, 32, look, (zero, zero, zero), unroll=8)
            tab[layer, i, 0] = first
            tab[layer, i, 1] = second
            tab[layer, i, 2] = sources[first]
            tab[layer, i, 3] = sources[second]
            tab[layer, i, 4] = seen

    def meta_copy(i):
        return remote(msg_out.at[i], msg_in.at[i], meta_s.at[i], meta_r.at[i], peer(i))

    def message(i):
        row = lax.broadcasted_iota(jnp.int32, (8, 128), 0)
        msg = jnp.zeros((8, 128), F32)
        for layer, targets in ((0, tgt1), (1, tgt2)):
            for k in range(2):
                e = tab[layer, i, k]
                used = tab[layer, i, 4] > k
                place = jnp.where(used, targets[e] * 16, -1024).astype(F32)
                msg = jnp.where(row == layer * 4 + k, cnt[layer, e], msg)
                msg = jnp.where(row == layer * 4 + 2 + k, place, msg)
        return msg

    def meta_send():
        msg_in[0] = message(0)

        @pl.loop(1, 32)
        def _(i):
            msg_out[i] = message(i)
            meta_copy(i).start()

    def meta_wait():
        @pl.loop(1, 32)
        def _(i):
            meta_copy(i).wait()

    def build(layer):
        @pl.loop(0, 32)
        def _(i):
            msg = msg_in[i]
            for k in range(2):
                rows = pl.ds(pl.multiple_of(i * 32 + k * 16, 16), 16)
                place = msg[layer * 4 + 2 + k : layer * 4 + 3 + k, :]
                vcol[rows, :] = jnp.broadcast_to(place, (16, 128))
                count = msg[layer * 4 + k : layer * 4 + k + 1, :]
                ccol[rows, :] = jnp.broadcast_to(count, (16, 128)).astype(BF)

        ramp = lax.broadcasted_iota(jnp.int32, (1024, 128), 0) % 16
        vrow = (vcol[...] + ramp.astype(F32)).T[0:1, :]
        spot = lax.broadcasted_iota(jnp.int32, (256, 1024), 0).astype(F32)
        lhs[layer] = jnp.where(spot == vrow, 1.0, 0.0).astype(BF)
        degree = dot(lhs[layer], ccol[...])
        lane = lax.broadcasted_iota(jnp.int32, (256, 128), 1)
        within = lax.broadcasted_iota(jnp.int32, (256, 128), 0) % 16
        for g in range(8):
            here = jnp.sum(jnp.where(lane == within + g * 16, degree, 0.0), axis=1, keepdims=True)
            rdeg[g] = jnp.broadcast_to(1.0 / jnp.maximum(here, 1.0), (256, 128))

    def piece_copy(phase, i):
        c = phase % 2
        return remote(
            sendbuf[c].at[i], recv[phase].at[i], aa_s.at[phase, i], aa_r.at[phase, i], peer(i)
        )

    def piece(layer, values, c, i, k):
        return dot(maskt[layer, tab[layer, i, k]], values[c][tab[layer, i, 2 + k]]).astype(BF)

    def pieces(phase, values):
        layer, c = phase // 2, phase % 2
        if layer == 1:

            @pl.loop(1, 32)
            def _(i):
                piece_copy(c, i).wait_send()

        @pl.loop(1, 32)
        def _(i):
            for k in range(2):
                sendbuf[c][i, k] = piece(layer, values, c, i, k)
            piece_copy(phase, i).start()

        for k in range(2):
            recv[phase][0, k] = piece(layer, values, c, 0, k)

    def gather_tiles(phase, result):
        layer, c = phase // 2, phase % 2

        @pl.loop(1, 32)
        def _(i):
            piece_copy(phase, i).wait_recv()

        for g in range(8):
            rows = pl.ds(g * 16, 16)
            got = recv[phase][:, :, rows, :].reshape(1024, 128)
            mean = dot(lhs[layer], got) * rdeg[g]
            if layer == 0:
                mean = jnp.maximum(own[2 + c, :, rows, :].reshape(256, 128) + mean, 0.0)
            result[c][:, rows, :] = mean.astype(BF).reshape(16, 16, 128)

    far = (right, left, opp)
    back = (1, 0, 2)

    def rows_copies(m, c, values):
        return [
            remote(
                values[c].at[pl.ds(d * 4, 4)], hm[m][c].at[f],
                rows_s.at[m, c, k], rows_r.at[m, c, k], (d, n),
            )
            for k, d in enumerate(far)
        ]

    def rows_send(m, c, values):
        start(rows_copies(m, c, values))
        hm[m][c][f] = values[c][pl.ds(f * 4, 4)]

    def rows_wait(m, c, values):
        for copy in rows_copies(m, c, values):
            copy.wait_recv()

    def cot_copies():
        return [
            remote(
                cot_hbm.at[pl.ds(pl.multiple_of(d * 512, 512), 512)], cot.at[f],
                cot_s.at[k], cot_r.at[k], (d, n),
            )
            for k, d in enumerate(far)
        ]

    def w2_copies(d, k):
        return remote(
            w2.at[core, f], w2.at[core, f], w2_s.at[k], w2_r.at[k], (d, n)
        )

    def w2_forward(d, k):
        return remote(
            w2.at[core, d], w2.at[core, d], wd_s.at[k], wd_r.at[k], (f, other)
        )

    def pre_add(m, c, first):
        left_side = jnp.concatenate([hm[m][c][s].reshape(512, 128) for s in range(4)], axis=1)

        @pl.loop(0, 4)
        def _(j):
            cols = pl.ds(pl.multiple_of(j * 256, 256), 256)
            part = dot(left_side, w2[m, :, c, :, cols].reshape(512, 256))
            for half in range(2):
                new = part[:, half * 128 : (half + 1) * 128].reshape(4, 128, 128)
                at = pl.ds(j * 4, 4)
                own[half, at] = new if first else own[half, at] + new

    def x_copy(c, m=0):
        return remote(hm[m][c], xoth[c], x_s.at[c], x_r.at[c], (f, other))

    def x_send(c):
        for m in range(2):

            @pl.when(core == 1 - m)
            def _():
                x_copy(c, m).start()

    def transpose_x(c):
        for m in range(2):

            @pl.when(core == m)
            def _():
                for s in range(4):
                    mine = hm[m][c][s].reshape(512, 128).astype(F32).T.astype(BF)
                    xt[c, s * 128 : (s + 1) * 128, 0:512] = mine

        x_copy(c).wait_recv()
        for s in range(4):
            theirs = xoth[c][s].reshape(512, 128).astype(F32).T.astype(BF)
            xt[c, s * 128 : (s + 1) * 128, 512:1024] = theirs

    def slope_copy():
        return remote(slope_own, slope_oth, sl_s.at[0], sl_r.at[0], (f, other))

    def h2_copies():
        return [
            remote(
                feat.at[pl.ds(pl.multiple_of(d * 512, 512), 512), pl.ds(0, 256)], hid2_out.at[pl.ds(pl.multiple_of(f * 512, 512), 512)],
                h2_s.at[k], h2_r.at[k], (d, n),
            )
            for k, d in enumerate(far)
        ]

    def along_y(d):
        return (f, z * 8 + ((y + d) % 4) * 2 + core)

    def along_z(d):
        return (f, ((z + d) % 4) * 8 + y * 2 + core)

    def g1_copies(h):
        out = []
        for d in (1, 2, 3):
            if h == 0:
                src, dev = g0.at[:, :, (y + d) % 4], along_y(d)
            else:
                src, dev = g1.at[:, (z + d) % 4], along_z(d)
            out.append(remote(src, r1[h].at[d - 1], g1_s.at[h, d - 1], g1_r.at[h, d - 1], dev))
        return out

    def g2_copies(h):
        out = []
        for d in (1, 2, 3):
            to = (z + d) % 4 if h == 0 else (y + d) % 4
            dev = along_z(d) if h == 0 else along_y(d)
            out.append(remote(s1[h].at[:, to], r2[h].at[d - 1], g2_s.at[h, d - 1], g2_r.at[h, d - 1], dev))
        return out

    def g3_copies(h):
        return [
            remote(
                s2[h].at[(f + d) % 4], r3[h].at[d - 1],
                g3_s.at[h, d - 1], g3_r.at[h, d - 1], ((f + d) % 4, n),
            )
            for d in (1, 2, 3)
        ]

    def fin_copy():
        rows = pl.ds(pl.multiple_of((1 - core) * 8, 8), 8)
        return remote(fin.at[rows], finr, fn_s.at[0], fn_r.at[0], (f, other))

    for c in [*loads, load_mask2]:
        c.wait()
    project(NEIGH, opp, 0)
    start(copies_a(0))
    project(NEIGH, right, 1)
    project(NEIGH, left, 2)
    start(copies_direct(0))
    project(NEIGH, f, None)
    slots_of(0, own1, src1)
    slots_of(1, own2, src2)
    masks_of(0, mask1)
    ring_add(0)
    ring_start(1)
    project(SELF, opp, 0)
    project(SELF, right, 1)
    project(SELF, left, 2)
    project(SELF, f, None)
    masks_of(1, mask2)
    meta_send()
    ring_end(0)
    pieces(0, proj)
    ring_add(1)
    ring_start(2)
    meta_wait()
    build(0)
    ring_end(1)
    pieces(1, proj)
    ring_add(2)
    ring_start(3)
    ring_end(2)
    gather_tiles(0, hid)
    pieces(2, hid)
    rows_send(0, 0, hid)
    ring_add(3)
    ring_end(3)
    gather_tiles(1, hid)
    pieces(3, hid)
    rows_send(0, 1, hid)
    build(1)
    start(cot_copies())
    for k, d in enumerate(far):
        w2_copies(d, k).start()
    rows_wait(0, 0, hid)
    rows_wait(0, 1, hid)
    for k in range(3):
        w2_copies(far[k], k).wait_recv()
    for k, d in enumerate(far):
        w2_forward(d, k).start()
    for k, d in enumerate(far):
        w2_forward(d, k).wait_recv()
    pre_add(0, 0, True)
    pre_add(0, 1, False)
    gather_tiles(2, proj)
    rows_send(1, 0, proj)
    rows_wait(1, 0, proj)
    x_send(0)
    pre_add(1, 0, False)
    transpose_x(0)
    gather_tiles(3, proj)
    rows_send(1, 1, proj)
    for c in cot_copies():
        c.wait_recv()
    rows_wait(1, 1, proj)
    x_send(1)
    pre_add(1, 1, False)
    for j in range(4):

        @pl.loop(0, 4)
        def _(t):
            rows = pl.ds(pl.multiple_of(t * 128, 128), 128)
            out_rows = pl.ds(pl.multiple_of(t * 128 + j * 512, 128), 128)
            for half in range(2):
                cols = slice(half * 128, (half + 1) * 128)
                v = own[half, j * 4 + t]
                s = 1.0 / (1.0 + jnp.exp(-v))
                feat[out_rows, cols] = (v * s).astype(BF)
                up = cot[j, rows, cols].astype(F32) * s * (1.0 + v * (1.0 - s))
                slope_own[j, rows, cols] = up.astype(BF)

    slope_copy().start()
    start(h2_copies())
    mine = pl.ds(pl.multiple_of(f * 512, 512), 512)
    hid2_out[mine, :] = feat[mine, 0:256]
    transpose_x(1)
    slope_copy().wait_recv()
    for j in range(4):
        up = jnp.concatenate([slope_own[j], slope_oth[j]], axis=0)
        grad = g0 if j < 2 else g1
        cols = pl.ds((j % 2) * 256, 256)
        for c in range(2):
            part = dot(xt[c], up).astype(BF)
            grad[:, 2 * c : 2 * c + 2, :, :, cols] = part.reshape(4, 2, 4, 16, 256)
        if j == 1:
            start(g1_copies(0))
        if j == 3:
            start(g1_copies(1))
    for h in range(2):
        for c in g1_copies(h):
            c.wait_recv()
        first = g0[:, :, y] if h == 0 else g1[:, z]
        total = first.astype(F32)
        for d in range(3):
            total = total + r1[h][d].astype(F32)
        s1[h][...] = total
        start(g2_copies(h))
    for h in range(2):
        for c in g2_copies(h):
            c.wait_recv()
        at = z if h == 0 else y
        s2[h][...] = s1[h][:, at] + r2[h][0] + r2[h][1] + r2[h][2]
        start(g3_copies(h))
    for h in range(2):
        for c in g3_copies(h):
            c.wait_recv()
        fin[:, h * 512 : (h + 1) * 512] = s2[h][f] + r3[h][0] + r3[h][1] + r3[h][2]
    fin_copy().start()
    fin_copy().wait_recv()
    mine8 = fin[pl.ds(pl.multiple_of(core * 8, 8), 8), :]
    first_core = jnp.full((8, 1024), core, jnp.int32) == 0
    gs_out[...] = jnp.where(first_core, mine8, finr[...])
    gn_out[...] = jnp.where(first_core, finr[...], mine8)

    for c in h2_copies():
        c.wait_recv()
    for q in range(4):
        for c in copies_a(q) + copies_direct(q) + copies_added(q):
            c.wait_send()

    @pl.loop(1, 32)
    def _(i):
        piece_copy(2, i).wait_send()
        piece_copy(3, i).wait_send()

    for m, values in ((0, hid), (1, proj)):
        for c in range(2):
            for copy in rows_copies(m, c, values):
                copy.wait_send()
    rest = cot_copies() + h2_copies() + [slope_copy(), fin_copy(), x_copy(0), x_copy(1)]
    for k, d in enumerate(far):
        rest += [w2_copies(d, k), w2_forward(d, k)]
    for h in range(2):
        rest += g1_copies(h) + g2_copies(h) + g3_copies(h)
    for copy in rest:
        copy.wait_send()


def local_step(
    features, self_w1, neigh_w1, self_w2, neigh_w2, source_tiles1, owner_blocks1, target_tiles1,
    tile_masks1, source_tiles2, owner_blocks2, target_tiles2, tile_masks2, cotangent,
):
    hbm = pl.BlockSpec(memory_space=pl.ANY)
    smem = pl.BlockSpec(memory_space=pltpu.SMEM)
    vmem = pl.BlockSpec(memory_space=pltpu.VMEM)
    v = pltpu.VMEM
    dma = pltpu.SemaphoreType.DMA

    def pair(*shape):
        return [dma(shape), dma(shape)]

    i32 = jnp.int32
    scratch = [
        v((2048, 512), BF), *[v((512, 1024), BF)] * 2, *[v((32, 128, 128), i32)] * 2,
        v((2, 32, 128, 128), BF), v((2, 32, 8, 128), F32), pltpu.SMEM((2, 32, 8), i32),
        *[v((3, 2048, 128), BF)] * 4, v((4, 16, 128, 128), F32), *[v((2, 1024, 128), BF)] * 4,
        *[v((2, 2048, 128), BF)] * 4, *[v((16, 128, 128), BF)] * 4,
        v((32, 8, 128), F32), v((32, 8, 128), F32), v((1024, 128), F32), v((1024, 128), BF),
        v((2, 256, 1024), BF), v((8, 256, 128), F32),
        *[v((32, 2, 128, 128), BF)] * 6, *[v((4, 4, 128, 128), BF)] * 6, v((2, 512, 1024), BF),
        v((4, 512, 256), BF), v((2, 4, 2, 128, 1024), BF), *[v((4, 512, 256), BF)] * 2,
        *[v((4, 4, 4, 16, 512), BF)] * 2, *[v((3, 4, 4, 16, 512), BF)] * 2,
        *[v((4, 4, 16, 512), F32)] * 2, *[v((3, 4, 16, 512), F32)] * 2, *[v((4, 16, 512), F32)] * 2,
        *[v((3, 16, 512), F32)] * 2, v((16, 1024), F32), v((8, 1024), F32),
        dma((10,)),
        *pair(32), *pair(4, 2), *pair(4, 4), *pair(4, 32), *pair(2, 2, 3), *pair(3), *pair(3),
        *pair(3), *pair(2), *pair(1), *pair(3), *pair(2, 3), *pair(2, 3), *pair(2, 3), *pair(1),
    ]
    hidden2, grad_self, grad_neigh = pl.pallas_call(
        kernel,
        out_shape=(
            jax.ShapeDtypeStruct((2048, 256), BF),
            jax.ShapeDtypeStruct((8, 1024), F32),
            jax.ShapeDtypeStruct((8, 1024), F32),
        ),
        in_specs=[hbm] * 5 + [smem] * 3 + [hbm] + [smem] * 3 + [hbm] * 2,
        out_specs=(vmem, vmem, vmem),
        scratch_shapes=scratch,
        compiler_params=pltpu.CompilerParams(
            collective_id=0, has_side_effects=True, vmem_limit_bytes=(64 << 20) - (64 << 10)
        ),
        cost_estimate=pl.CostEstimate(flops=10**10, bytes_accessed=16 << 20, transcendentals=1 << 19),
        name="sage",
    )(
        features, self_w1, neigh_w1, self_w2, neigh_w2, source_tiles1, owner_blocks1, target_tiles1,
        tile_masks1, source_tiles2, owner_blocks2, target_tiles2, tile_masks2, cotangent,
    )
    return hidden2, grad_self, grad_neigh


def solution(mesh):
    node3 = P("node", None, None)
    in_specs = (
        P("node", "feat"), P("feat", None), P("feat", None), P("feat", None), P("feat", None),
        P("node"), P("node", None), P("node"), node3,
        P("node"), P("node", None), P("node"), node3, P("node", "feat"),
    )
    out_specs = (P("node", "feat"), P(("feat", "node"), None), P(("feat", "node"), None))
    return jax.shard_map(local_step, mesh=mesh, in_specs=in_specs, out_specs=out_specs, check_vma=False)
```

```python
import functools

import jax
import jax.numpy as jnp
from jax import lax
from jax.experimental import pallas as pl
from jax.experimental.pallas import tpu as pltpu
from jax.sharding import PartitionSpec as P

MESH = pl.DeviceIdType.MESH
BF = jnp.bfloat16
F32 = jnp.float32
NEIGH, SELF = 0, 1


def dot(a, b):
    return jnp.dot(a, b, preferred_element_type=F32)


def kernel(
    feat_hbm, ws1_hbm, wn1_hbm, ws2_hbm, wn2_hbm,
    src1, tgt1, mask1_hbm, src2, tgt2, mask2_hbm, owners, cot_hbm,
    hid2_out, gs_out, gn_out,
    feat, w1n, w1s, mask1, mask2, maskt, cnt, tab,
    p0, p1, p2, p3, own, a0, a1, a2, a3, b0, b1, b2, b3, proj0, proj1, hid0, hid1,
    msg_out, msg_in, vcol, ccol, lhs, rdeg,
    send0, send1, recv0, recv1, recv2, recv3, h0, h1, m0, m1, xoth0, xoth1, xt,
    cot, w2, slope_own, slope_oth,
    g0, g1, r1a, r1b, s1a, s1b, r2a, r2b, s2a, s2b, r3a, r3b, fin, finr,
    ld, meta_s, meta_r, ra_s, ra_r, rb_s, rb_r, aa_s, aa_r, rows_s, rows_r,
    cot_s, cot_r, w2_s, w2_r, wd_s, wd_r, x_s, x_r, sl_s, sl_r, h2_s, h2_r,
    g1_s, g1_r, g2_s, g2_r, g3_s, g3_r, fn_s, fn_r,
):
    f = lax.axis_index("feat")
    n = lax.axis_index("node")
    z, y, core = n // 8, (n // 2) % 4, n % 2
    sign = 1 - 2 * core
    right, left, opp = (f + 1) % 4, (f + 3) % 4, (f + 2) % 4
    other = n + sign
    proj, hid = (proj0, proj1), (hid0, hid1)
    psend, buf_a, buf_b = (p0, p1, p2, p3), (a0, a1, a2, a3), (b0, b1, b2, b3)
    sendbuf, recv = (send0, send1), (recv0, recv1, recv2, recv3)
    hm, xoth = ((h0, h1), (m0, m1)), (xoth0, xoth1)
    r1, s1, r2, s2, r3 = (r1a, r1b), (s1a, s1b), (r2a, r2b), (s2a, s2b), (r3a, r3b)

    def peer(i):
        j, ii, dc = i // 8, (i // 2) % 4, i % 2
        zz = (z + sign * ii + 4) % 4
        yy = (y + sign * ((ii + j) % 4) + 4) % 4
        return (f, zz * 8 + yy * 2 + (core + dc) % 2)

    def remote(src, dst, ss, rs, dev):
        return pltpu.make_async_remote_copy(
            src_ref=src, dst_ref=dst, send_sem=ss, recv_sem=rs, device_id=dev, device_id_type=MESH
        )

    def local(src, dst, k):
        return pltpu.make_async_copy(src, dst, ld.at[k])

    loads = [
        local(feat_hbm, feat, 0),
        local(wn1_hbm, w1n, 1),
        local(ws1_hbm, w1s, 2),
        local(mask1_hbm, mask1, 3),
        local(cot_hbm.at[pl.ds(pl.multiple_of(f * 512, 512), 512)], cot.at[f], 4),
    ]
    for m, ref in ((0, ws2_hbm), (1, wn2_hbm)):
        for c in range(2):
            loads.append(local(ref.at[pl.ds(c * 128, 128)], w2.at[m, f, c], 5 + 2 * m + c))
    load_mask2 = local(mask2_hbm, mask2, 9)
    for c in [*loads, load_mask2]:
        c.start()

    barrier = pltpu.get_barrier_semaphore()

    @pl.loop(1, 32)
    def _(i):
        pl.semaphore_signal(barrier, inc=1, device_id=peer(i), device_id_type=MESH)

    for d in (right, left, opp):
        pl.semaphore_signal(barrier, inc=1, device_id=(d, n), device_id_type=MESH)
    pl.semaphore_wait(barrier, 34)

    def project(mat, j, where):
        cols = pl.ds(pl.multiple_of(j * 256, 256), 256)

        @pl.loop(0, 4)
        def _(t):
            rows = pl.ds(pl.multiple_of(t * 512, 512), 512)
            part = dot(feat[rows, :], (w1n, w1s)[mat][:, cols])
            for c in range(2):
                half = part[:, c * 128 : (c + 1) * 128]
                if where is None:
                    own[2 * mat + c, pl.ds(t * 4, 4)] = half.reshape(4, 128, 128)
                else:
                    psend[2 * mat + c][where, rows, :] = half.astype(BF)

    lo, hi = pl.ds(0, 1024), pl.ds(1024, 1024)

    def copies_a(q):
        return [
            remote(psend[q].at[0, lo], buf_a[q].at[0], ra_s.at[q, 0], ra_r.at[q, 0], (right, n)),
            remote(psend[q].at[0, hi], buf_a[q].at[1], ra_s.at[q, 1], ra_r.at[q, 1], (left, n)),
        ]

    def copies_direct(q):
        return [
            remote(psend[q].at[1, hi], buf_b[q].at[0, hi], rb_s.at[q, 0], rb_r.at[q, 0], (right, n)),
            remote(psend[q].at[2, lo], buf_b[q].at[1, lo], rb_s.at[q, 1], rb_r.at[q, 1], (left, n)),
        ]

    def copies_added(q):
        return [
            remote(psend[q].at[1, lo], buf_b[q].at[0, lo], rb_s.at[q, 2], rb_r.at[q, 2], (right, n)),
            remote(psend[q].at[2, hi], buf_b[q].at[1, hi], rb_s.at[q, 3], rb_r.at[q, 3], (left, n)),
        ]

    def start(copies):
        for c in copies:
            c.start()

    def ring_add(q):
        a, b = copies_a(q), copies_added(q)
        for s, base in ((0, 0), (1, 1024)):
            a[s].wait_recv()

            @pl.loop(0, 4)
            def _(t):
                rows = pl.ds(pl.multiple_of(t * 256 + base, 256), 256)
                from_rows = pl.ds(pl.multiple_of(t * 256, 256), 256)
                total = psend[q][1 + s, rows, :].astype(F32) + buf_a[q][s, from_rows, :].astype(F32)
                psend[q][1 + s, rows, :] = total.astype(BF)

            b[s].start()

    def ring_end(q):
        for c in copies_direct(q) + copies_added(q):
            c.wait_recv()

        @pl.loop(0, 8)
        def _(t):
            rows = pl.ds(pl.multiple_of(t * 256, 256), 256)
            got = buf_b[q][0, rows, :].astype(F32) + buf_b[q][1, rows, :].astype(F32)
            total = own[q, pl.ds(t * 2, 2)] + got.reshape(2, 128, 128)
            if q < 2:
                proj[q][pl.ds(t * 2, 2)] = total.astype(BF)
            else:
                own[q, pl.ds(t * 2, 2)] = total

    def masks_of(layer, mask):
        @pl.loop(0, 32)
        def _(e):
            m = mask[e].astype(F32)
            cnt[layer, e] = jnp.broadcast_to(jnp.sum(m, axis=0, keepdims=True), (8, 128))
            maskt[layer, e] = m.T.astype(BF)

    def slots_of(layer, sources):
        @pl.loop(0, 32)
        def _(i):
            who = peer(i)[1]

            def look(e, carry):
                seen, first, second = carry
                hit = owners[layer * 32 + e] == who
                first = jnp.where(jnp.logical_and(hit, seen == 0), e, first)
                second = jnp.where(jnp.logical_and(hit, seen == 1), e, second)
                return seen + hit.astype(jnp.int32), first, second

            zero = jnp.int32(0)
            seen, first, second = lax.fori_loop(0, 32, look, (zero, zero, zero), unroll=8)
            tab[layer, i, 0] = first
            tab[layer, i, 1] = second
            tab[layer, i, 2] = sources[first]
            tab[layer, i, 3] = sources[second]
            tab[layer, i, 4] = seen

    def meta_copy(i):
        return remote(msg_out.at[i], msg_in.at[i], meta_s.at[i], meta_r.at[i], peer(i))

    def message(i):
        row = lax.broadcasted_iota(jnp.int32, (8, 128), 0)
        msg = jnp.zeros((8, 128), F32)
        for layer, targets in ((0, tgt1), (1, tgt2)):
            for k in range(2):
                e = tab[layer, i, k]
                used = tab[layer, i, 4] > k
                place = jnp.where(used, targets[e] * 16, -1024).astype(F32)
                msg = jnp.where(row == layer * 4 + k, cnt[layer, e], msg)
                msg = jnp.where(row == layer * 4 + 2 + k, place, msg)
        return msg

    def meta_send():
        msg_in[0] = message(0)

        @pl.loop(1, 32)
        def _(i):
            msg_out[i] = message(i)
            meta_copy(i).start()

    def meta_wait():
        @pl.loop(1, 32)
        def _(i):
            meta_copy(i).wait()

    def build(layer):
        @pl.loop(0, 32)
        def _(i):
            msg = msg_in[i]
            for k in range(2):
                rows = pl.ds(pl.multiple_of(i * 32 + k * 16, 16), 16)
                place = msg[layer * 4 + 2 + k : layer * 4 + 3 + k, :]
                vcol[rows, :] = jnp.broadcast_to(place, (16, 128))
                count = msg[layer * 4 + k : layer * 4 + k + 1, :]
                ccol[rows, :] = jnp.broadcast_to(count, (16, 128)).astype(BF)

        ramp = lax.broadcasted_iota(jnp.int32, (1024, 128), 0) % 16
        vrow = (vcol[...] + ramp.astype(F32)).T[0:1, :]
        spot = lax.broadcasted_iota(jnp.int32, (256, 1024), 0).astype(F32)
        lhs[layer] = jnp.where(spot == vrow, 1.0, 0.0).astype(BF)
        degree = dot(lhs[layer], ccol[...])
        lane = lax.broadcasted_iota(jnp.int32, (256, 128), 1)
        within = lax.broadcasted_iota(jnp.int32, (256, 128), 0) % 16
        for g in range(8):
            here = jnp.sum(jnp.where(lane == within + g * 16, degree, 0.0), axis=1, keepdims=True)
            rdeg[g] = jnp.broadcast_to(1.0 / jnp.maximum(here, 1.0), (256, 128))

    def piece_copy(phase, i):
        c = phase % 2
        return remote(
            sendbuf[c].at[i], recv[phase].at[i], aa_s.at[phase, i], aa_r.at[phase, i], peer(i)
        )

    def piece(layer, values, c, i, k):
        return dot(maskt[layer, tab[layer, i, k]], values[c][tab[layer, i, 2 + k]]).astype(BF)

    def pieces(phase, values):
        layer, c = phase // 2, phase % 2
        if layer == 1:

            @pl.loop(1, 32)
            def _(i):
                piece_copy(c, i).wait_send()

        @pl.loop(1, 32)
        def _(i):
            for k in range(2):
                sendbuf[c][i, k] = piece(layer, values, c, i, k)
            piece_copy(phase, i).start()

        for k in range(2):
            recv[phase][0, k] = piece(layer, values, c, 0, k)

    def gather_tiles(phase, result):
        layer, c = phase // 2, phase % 2

        @pl.loop(1, 32)
        def _(i):
            piece_copy(phase, i).wait_recv()

        for g in range(8):
            rows = pl.ds(g * 16, 16)
            got = recv[phase][:, :, rows, :].reshape(1024, 128)
            mean = dot(lhs[layer], got) * rdeg[g]
            if layer == 0:
                mean = jnp.maximum(own[2 + c, :, rows, :].reshape(256, 128) + mean, 0.0)
            result[c][:, rows, :] = mean.astype(BF).reshape(16, 16, 128)

    far = (right, left, opp)
    back = (1, 0, 2)

    def rows_copies(m, c, values):
        return [
            remote(
                values[c].at[pl.ds(d * 4, 4)], hm[m][c].at[f],
                rows_s.at[m, c, k], rows_r.at[m, c, k], (d, n),
            )
            for k, d in enumerate(far)
        ]

    def rows_send(m, c, values):
        start(rows_copies(m, c, values))
        hm[m][c][f] = values[c][pl.ds(f * 4, 4)]

    def rows_wait(m, c, values):
        for copy in rows_copies(m, c, values):
            copy.wait_recv()

    def cot_copies():
        return [
            remote(
                cot_hbm.at[pl.ds(pl.multiple_of(d * 512, 512), 512)], cot.at[f],
                cot_s.at[k], cot_r.at[k], (d, n),
            )
            for k, d in enumerate(far)
        ]

    def w2_copies(d, k):
        return remote(
            w2.at[core, f], w2.at[core, f], w2_s.at[k], w2_r.at[k], (d, n)
        )

    def w2_forward(d, k):
        return remote(
            w2.at[core, d], w2.at[core, d], wd_s.at[k], wd_r.at[k], (f, other)
        )

    def pre_add(m, c, first):
        left_side = jnp.concatenate([hm[m][c][s].reshape(512, 128) for s in range(4)], axis=1)

        @pl.loop(0, 4)
        def _(j):
            cols = pl.ds(pl.multiple_of(j * 256, 256), 256)
            part = dot(left_side, w2[m, :, c, :, cols].reshape(512, 256))
            for half in range(2):
                new = part[:, half * 128 : (half + 1) * 128].reshape(4, 128, 128)
                at = pl.ds(j * 4, 4)
                own[half, at] = new if first else own[half, at] + new

    def x_copy(c, m=0):
        return remote(hm[m][c], xoth[c], x_s.at[c], x_r.at[c], (f, other))

    def x_send(c):
        for m in range(2):

            @pl.when(core == 1 - m)
            def _():
                x_copy(c, m).start()

    def transpose_x(c):
        for m in range(2):

            @pl.when(core == m)
            def _():
                for s in range(4):
                    mine = hm[m][c][s].reshape(512, 128).astype(F32).T.astype(BF)
                    xt[c, s * 128 : (s + 1) * 128, 0:512] = mine

        x_copy(c).wait_recv()
        for s in range(4):
            theirs = xoth[c][s].reshape(512, 128).astype(F32).T.astype(BF)
            xt[c, s * 128 : (s + 1) * 128, 512:1024] = theirs

    def slope_copy():
        return remote(slope_own, slope_oth, sl_s.at[0], sl_r.at[0], (f, other))

    def h2_copies():
        return [
            remote(
                feat.at[pl.ds(pl.multiple_of(d * 512, 512), 512), pl.ds(0, 256)], hid2_out.at[pl.ds(pl.multiple_of(f * 512, 512), 512)],
                h2_s.at[k], h2_r.at[k], (d, n),
            )
            for k, d in enumerate(far)
        ]

    def along_y(d):
        return (f, z * 8 + ((y + d) % 4) * 2 + core)

    def along_z(d):
        return (f, ((z + d) % 4) * 8 + y * 2 + core)

    def g1_copies(h):
        out = []
        for d in (1, 2, 3):
            if h == 0:
                src, dev = g0.at[:, :, (y + d) % 4], along_y(d)
            else:
                src, dev = g1.at[:, (z + d) % 4], along_z(d)
            out.append(remote(src, r1[h].at[d - 1], g1_s.at[h, d - 1], g1_r.at[h, d - 1], dev))
        return out

    def g2_copies(h):
        out = []
        for d in (1, 2, 3):
            to = (z + d) % 4 if h == 0 else (y + d) % 4
            dev = along_z(d) if h == 0 else along_y(d)
            out.append(remote(s1[h].at[:, to], r2[h].at[d - 1], g2_s.at[h, d - 1], g2_r.at[h, d - 1], dev))
        return out

    def g3_copies(h):
        return [
            remote(
                s2[h].at[(f + d) % 4], r3[h].at[d - 1],
                g3_s.at[h, d - 1], g3_r.at[h, d - 1], ((f + d) % 4, n),
            )
            for d in (1, 2, 3)
        ]

    def fin_copy():
        rows = pl.ds(pl.multiple_of((1 - core) * 8, 8), 8)
        return remote(fin.at[rows], finr, fn_s.at[0], fn_r.at[0], (f, other))

    loads[0].wait()
    loads[1].wait()
    project(NEIGH, opp, 0)
    start(copies_a(0))
    project(NEIGH, right, 1)
    project(NEIGH, left, 2)
    start(copies_direct(0))
    start(copies_a(1))
    project(NEIGH, f, None)
    for c in loads[2:]:
        c.wait()
    masks_of(0, mask1)
    ring_add(0)
    start(copies_direct(1))
    slots_of(0, src1)
    project(SELF, opp, 0)
    ring_add(1)
    start(copies_a(2))
    project(SELF, right, 1)
    project(SELF, left, 2)
    start(copies_direct(2))
    project(SELF, f, None)
    ring_end(0)
    pieces(0, proj)
    load_mask2.wait()
    masks_of(1, mask2)
    slots_of(1, src2)
    meta_send()
    start(copies_a(3))
    ring_end(1)
    pieces(1, proj)
    ring_add(2)
    start(copies_direct(3))
    meta_wait()
    build(0)
    ring_add(3)
    ring_end(2)
    gather_tiles(0, hid)
    pieces(2, hid)
    rows_send(0, 0, hid)
    for k, d in enumerate(far):
        w2_copies(d, k).start()
    start(cot_copies())
    ring_end(3)
    gather_tiles(1, hid)
    pieces(3, hid)
    rows_send(0, 1, hid)
    build(1)
    for k in range(3):
        w2_copies(far[k], k).wait_recv()
    for k, d in enumerate(far):
        w2_forward(d, k).start()
    rows_wait(0, 0, hid)
    rows_wait(0, 1, hid)
    for k, d in enumerate(far):
        w2_forward(d, k).wait_recv()
    pre_add(0, 0, True)
    pre_add(0, 1, False)
    gather_tiles(2, proj)
    rows_send(1, 0, proj)
    rows_wait(1, 0, proj)
    x_send(0)
    pre_add(1, 0, False)
    transpose_x(0)
    gather_tiles(3, proj)
    rows_send(1, 1, proj)
    for c in cot_copies():
        c.wait_recv()
    rows_wait(1, 1, proj)
    x_send(1)
    pre_add(1, 1, False)
    for j in range(4):

        @pl.loop(0, 4)
        def _(t):
            rows = pl.ds(pl.multiple_of(t * 128, 128), 128)
            out_rows = pl.ds(pl.multiple_of(t * 128 + j * 512, 128), 128)
            for half in range(2):
                cols = slice(half * 128, (half + 1) * 128)
                v = own[half, j * 4 + t]
                s = 1.0 / (1.0 + jnp.exp(-v))
                feat[out_rows, cols] = (v * s).astype(BF)
                up = cot[j, rows, cols].astype(F32) * s * (1.0 + v * (1.0 - s))
                slope_own[j, rows, cols] = up.astype(BF)

    slope_copy().start()
    start(h2_copies())
    mine = pl.ds(pl.multiple_of(f * 512, 512), 512)
    hid2_out[mine, :] = feat[mine, 0:256]
    transpose_x(1)
    slope_copy().wait_recv()
    for j in range(4):
        up = jnp.concatenate([slope_own[j], slope_oth[j]], axis=0)
        grad = g0 if j < 2 else g1
        cols = pl.ds((j % 2) * 256, 256)
        for c in range(2):
            part = dot(xt[c], up).astype(BF)
            grad[:, 2 * c : 2 * c + 2, :, :, cols] = part.reshape(4, 2, 4, 16, 256)
        if j == 1:
            start(g1_copies(0))
        if j == 3:
            start(g1_copies(1))
    for h in range(2):
        for c in g1_copies(h):
            c.wait_recv()
        first = g0[:, :, y] if h == 0 else g1[:, z]
        total = first.astype(F32)
        for d in range(3):
            total = total + r1[h][d].astype(F32)
        s1[h][...] = total
        start(g2_copies(h))
    for h in range(2):
        for c in g2_copies(h):
            c.wait_recv()
        at = z if h == 0 else y
        s2[h][...] = s1[h][:, at] + r2[h][0] + r2[h][1] + r2[h][2]
        start(g3_copies(h))
    for h in range(2):
        for c in g3_copies(h):
            c.wait_recv()
        fin[:, h * 512 : (h + 1) * 512] = s2[h][f] + r3[h][0] + r3[h][1] + r3[h][2]
    fin_copy().start()
    fin_copy().wait_recv()
    mine8 = fin[pl.ds(pl.multiple_of(core * 8, 8), 8), :]
    first_core = jnp.full((8, 1024), core, jnp.int32) == 0
    gs_out[...] = jnp.where(first_core, mine8, finr[...])
    gn_out[...] = jnp.where(first_core, finr[...], mine8)

    for c in h2_copies():
        c.wait_recv()
    for q in range(4):
        for c in copies_a(q) + copies_direct(q) + copies_added(q):
            c.wait_send()

    @pl.loop(1, 32)
    def _(i):
        piece_copy(2, i).wait_send()
        piece_copy(3, i).wait_send()

    for m, values in ((0, hid), (1, proj)):
        for c in range(2):
            for copy in rows_copies(m, c, values):
                copy.wait_send()
    rest = cot_copies() + h2_copies() + [slope_copy(), fin_copy(), x_copy(0), x_copy(1)]
    for k, d in enumerate(far):
        rest += [w2_copies(d, k), w2_forward(d, k)]
    for h in range(2):
        rest += g1_copies(h) + g2_copies(h) + g3_copies(h)
    for copy in rest:
        copy.wait_send()


def local_step(
    features, self_w1, neigh_w1, self_w2, neigh_w2, source_tiles1, owner_blocks1, target_tiles1,
    tile_masks1, source_tiles2, owner_blocks2, target_tiles2, tile_masks2, cotangent,
):
    hbm = pl.BlockSpec(memory_space=pl.ANY)
    smem = pl.BlockSpec(memory_space=pltpu.SMEM)
    vmem = pl.BlockSpec(memory_space=pltpu.VMEM)
    v = pltpu.VMEM
    dma = pltpu.SemaphoreType.DMA

    def pair(*shape):
        return [dma(shape), dma(shape)]

    i32 = jnp.int32
    scratch = [
        v((2048, 512), BF), *[v((512, 1024), BF)] * 2, *[v((32, 128, 128), i32)] * 2,
        v((2, 32, 128, 128), BF), v((2, 32, 8, 128), F32), pltpu.SMEM((2, 32, 8), i32),
        *[v((3, 2048, 128), BF)] * 4, v((4, 16, 128, 128), F32), *[v((2, 1024, 128), BF)] * 4,
        *[v((2, 2048, 128), BF)] * 4, *[v((16, 128, 128), BF)] * 4,
        v((32, 8, 128), F32), v((32, 8, 128), F32), v((1024, 128), F32), v((1024, 128), BF),
        v((2, 256, 1024), BF), v((8, 256, 128), F32),
        *[v((32, 2, 128, 128), BF)] * 6, *[v((4, 4, 128, 128), BF)] * 6, v((2, 512, 1024), BF),
        v((4, 512, 256), BF), v((2, 4, 2, 128, 1024), BF), *[v((4, 512, 256), BF)] * 2,
        *[v((4, 4, 4, 16, 512), BF)] * 2, *[v((3, 4, 4, 16, 512), BF)] * 2,
        *[v((4, 4, 16, 512), F32)] * 2, *[v((3, 4, 16, 512), F32)] * 2, *[v((4, 16, 512), F32)] * 2,
        *[v((3, 16, 512), F32)] * 2, v((16, 1024), F32), v((8, 1024), F32),
        dma((10,)),
        *pair(32), *pair(4, 2), *pair(4, 4), *pair(4, 32), *pair(2, 2, 3), *pair(3), *pair(3),
        *pair(3), *pair(2), *pair(1), *pair(3), *pair(2, 3), *pair(2, 3), *pair(2, 3), *pair(1),
    ]
    hidden2, grad_self, grad_neigh = pl.pallas_call(
        kernel,
        out_shape=(
            jax.ShapeDtypeStruct((2048, 256), BF),
            jax.ShapeDtypeStruct((8, 1024), F32),
            jax.ShapeDtypeStruct((8, 1024), F32),
        ),
        in_specs=[hbm] * 5 + [smem] * 2 + [hbm] + [smem] * 2 + [hbm, smem, hbm],
        out_specs=(vmem, vmem, vmem),
        scratch_shapes=scratch,
        compiler_params=pltpu.CompilerParams(
            collective_id=0, has_side_effects=True, vmem_limit_bytes=(64 << 20) - (64 << 10)
        ),
        cost_estimate=pl.CostEstimate(flops=10**10, bytes_accessed=16 << 20, transcendentals=1 << 19),
        name="sage",
    )(
        features, self_w1, neigh_w1, self_w2, neigh_w2, source_tiles1, target_tiles1, tile_masks1,
        source_tiles2, target_tiles2, tile_masks2,
        jnp.concatenate([owner_blocks1[:, 0], owner_blocks2[:, 0]]), cotangent,
    )
    return hidden2, grad_self, grad_neigh


def solution(mesh):
    node3 = P("node", None, None)
    in_specs = (
        P("node", "feat"), P("feat", None), P("feat", None), P("feat", None), P("feat", None),
        P("node"), P("node", None), P("node"), node3,
        P("node"), P("node", None), P("node"), node3, P("node", "feat"),
    )
    out_specs = (P("node", "feat"), P(("feat", "node"), None), P(("feat", "node"), None))
    return jax.shard_map(local_step, mesh=mesh, in_specs=in_specs, out_specs=out_specs, check_vma=False)
```

```python
import functools

import jax
import jax.numpy as jnp
from jax import lax
from jax.experimental import pallas as pl
from jax.experimental.pallas import tpu as pltpu
from jax.sharding import PartitionSpec as P

MESH = pl.DeviceIdType.MESH
BF = jnp.bfloat16
F32 = jnp.float32
NEIGH, SELF = 0, 1


def dot(a, b):
    return jnp.dot(a, b, preferred_element_type=F32)


def kernel(
    feat_hbm, ws1_hbm, wn1_hbm, ws2_hbm, wn2_hbm,
    src1, tgt1, mask1_hbm, src2, tgt2, mask2_hbm, owners, cot_hbm,
    hid2_out, gs_out, gn_out,
    feat, w1n, w1s, mask1, mask2, maskt, cnt, tab,
    p0, p1, p2, p3, own, a0, a1, a2, a3, b0, b1, b2, b3, proj0, proj1, hid0, hid1,
    msg_out, msg_in, vcol, ccol, lhs, rdeg,
    send0, send1, recv0, recv1, recv2, recv3, h0, h1, m0, m1, xoth0, xoth1, xt,
    cot, w2, wx, slope_own, slope_oth,
    g0, g1, r1a, r1b, s1a, s1b, r2a, r2b, s2a, s2b, r3a, r3b, fin, finr,
    ld, meta_s, meta_r, ra_s, ra_r, rb_s, rb_r, aa_s, aa_r, rows_s, rows_r,
    cot_s, cot_r, w2_s, w2_r, ws_s, ws_r, wd_s, wd_r, x_s, x_r, sl_s, sl_r, h2_s, h2_r,
    g1_s, g1_r, g2_s, g2_r, g3_s, g3_r, fn_s, fn_r,
):
    f = lax.axis_index("feat")
    n = lax.axis_index("node")
    z, y, core = n // 8, (n // 2) % 4, n % 2
    sign = 1 - 2 * core
    right, left, opp = (f + 1) % 4, (f + 3) % 4, (f + 2) % 4
    other = n + sign
    proj, hid = (proj0, proj1), (hid0, hid1)
    psend, buf_a, buf_b = (p0, p1, p2, p3), (a0, a1, a2, a3), (b0, b1, b2, b3)
    sendbuf, recv = (send0, send1), (recv0, recv1, recv2, recv3)
    hm, xoth = ((h0, h1), (m0, m1)), (xoth0, xoth1)
    r1, s1, r2, s2, r3 = (r1a, r1b), (s1a, s1b), (r2a, r2b), (s2a, s2b), (r3a, r3b)

    def peer(i):
        j, ii, dc = i // 8, (i // 2) % 4, i % 2
        zz = (z + sign * ii + 4) % 4
        yy = (y + sign * ((ii + j) % 4) + 4) % 4
        return (f, zz * 8 + yy * 2 + (core + dc) % 2)

    def remote(src, dst, ss, rs, dev):
        return pltpu.make_async_remote_copy(
            src_ref=src, dst_ref=dst, send_sem=ss, recv_sem=rs, device_id=dev, device_id_type=MESH
        )

    def local(src, dst, k):
        return pltpu.make_async_copy(src, dst, ld.at[k])

    loads = [
        local(feat_hbm, feat, 0),
        local(wn1_hbm, w1n, 1),
        local(ws1_hbm, w1s, 2),
        local(mask1_hbm, mask1, 3),
        local(cot_hbm.at[pl.ds(pl.multiple_of(f * 512, 512), 512)], cot.at[f], 4),
    ]
    for m, ref in ((0, ws2_hbm), (1, wn2_hbm)):
        loads.append(local(ref, w2.at[m, f], 5 + m))
    load_mask2 = local(mask2_hbm, mask2, 9)
    for c in [*loads, load_mask2]:
        c.start()

    barrier = pltpu.get_barrier_semaphore()

    @pl.loop(1, 32)
    def _(i):
        pl.semaphore_signal(barrier, inc=1, device_id=peer(i), device_id_type=MESH)

    for d in (right, left, opp):
        pl.semaphore_signal(barrier, inc=1, device_id=(d, n), device_id_type=MESH)
    pl.semaphore_wait(barrier, 34)

    def project(mat, j, where):
        cols = pl.ds(pl.multiple_of(j * 256, 256), 256)

        @pl.loop(0, 4)
        def _(t):
            rows = pl.ds(pl.multiple_of(t * 512, 512), 512)
            part = dot(feat[rows, :], (w1n, w1s)[mat][:, cols])
            for c in range(2):
                half = part[:, c * 128 : (c + 1) * 128]
                if where is None:
                    own[2 * mat + c, pl.ds(t * 4, 4)] = half.reshape(4, 128, 128)
                else:
                    psend[2 * mat + c][where, rows, :] = half.astype(BF)

    lo, hi = pl.ds(0, 1024), pl.ds(1024, 1024)

    def copies_a(q):
        return [
            remote(psend[q].at[0, lo], buf_a[q].at[0], ra_s.at[q, 0], ra_r.at[q, 0], (right, n)),
            remote(psend[q].at[0, hi], buf_a[q].at[1], ra_s.at[q, 1], ra_r.at[q, 1], (left, n)),
        ]

    def copies_direct(q):
        return [
            remote(psend[q].at[1, hi], buf_b[q].at[0, hi], rb_s.at[q, 0], rb_r.at[q, 0], (right, n)),
            remote(psend[q].at[2, lo], buf_b[q].at[1, lo], rb_s.at[q, 1], rb_r.at[q, 1], (left, n)),
        ]

    def copies_added(q):
        return [
            remote(psend[q].at[1, lo], buf_b[q].at[0, lo], rb_s.at[q, 2], rb_r.at[q, 2], (right, n)),
            remote(psend[q].at[2, hi], buf_b[q].at[1, hi], rb_s.at[q, 3], rb_r.at[q, 3], (left, n)),
        ]

    def start(copies):
        for c in copies:
            c.start()

    def ring_add(q):
        a, b = copies_a(q), copies_added(q)
        for s, base in ((0, 0), (1, 1024)):
            a[s].wait_recv()

            @pl.loop(0, 4)
            def _(t):
                rows = pl.ds(pl.multiple_of(t * 256 + base, 256), 256)
                from_rows = pl.ds(pl.multiple_of(t * 256, 256), 256)
                total = psend[q][1 + s, rows, :].astype(F32) + buf_a[q][s, from_rows, :].astype(F32)
                psend[q][1 + s, rows, :] = total.astype(BF)

            b[s].start()

    def ring_end(q):
        for c in copies_direct(q) + copies_added(q):
            c.wait_recv()

        @pl.loop(0, 8)
        def _(t):
            rows = pl.ds(pl.multiple_of(t * 256, 256), 256)
            got = buf_b[q][0, rows, :].astype(F32) + buf_b[q][1, rows, :].astype(F32)
            total = own[q, pl.ds(t * 2, 2)] + got.reshape(2, 128, 128)
            if q < 2:
                proj[q][pl.ds(t * 2, 2)] = total.astype(BF)
            else:
                own[q, pl.ds(t * 2, 2)] = total

    def masks_of(layer, mask):
        @pl.loop(0, 32)
        def _(e):
            m = mask[e].astype(F32)
            cnt[layer, e] = jnp.broadcast_to(jnp.sum(m, axis=0, keepdims=True), (8, 128))
            maskt[layer, e] = m.T.astype(BF)

    def slots_of(layer, sources):
        @pl.loop(0, 32)
        def _(i):
            who = peer(i)[1]

            def look(e, carry):
                seen, first, second = carry
                hit = owners[layer * 32 + e] == who
                first = jnp.where(jnp.logical_and(hit, seen == 0), e, first)
                second = jnp.where(jnp.logical_and(hit, seen == 1), e, second)
                return seen + hit.astype(jnp.int32), first, second

            zero = jnp.int32(0)
            seen, first, second = lax.fori_loop(0, 32, look, (zero, zero, zero), unroll=8)
            tab[layer, i, 0] = first
            tab[layer, i, 1] = second
            tab[layer, i, 2] = sources[first]
            tab[layer, i, 3] = sources[second]
            tab[layer, i, 4] = seen

    def meta_copy(i):
        return remote(msg_out.at[i], msg_in.at[i], meta_s.at[i], meta_r.at[i], peer(i))

    def message(i):
        row = lax.broadcasted_iota(jnp.int32, (8, 128), 0)
        msg = jnp.zeros((8, 128), F32)
        for layer, targets in ((0, tgt1), (1, tgt2)):
            for k in range(2):
                e = tab[layer, i, k]
                used = tab[layer, i, 4] > k
                place = jnp.where(used, targets[e] * 16, -1024).astype(F32)
                msg = jnp.where(row == layer * 4 + k, cnt[layer, e], msg)
                msg = jnp.where(row == layer * 4 + 2 + k, place, msg)
        return msg

    def meta_send():
        msg_in[0] = message(0)

        @pl.loop(1, 32)
        def _(i):
            msg_out[i] = message(i)
            meta_copy(i).start()

    def meta_wait():
        @pl.loop(1, 32)
        def _(i):
            meta_copy(i).wait()

    def build(layer):
        @pl.loop(0, 32)
        def _(i):
            msg = msg_in[i]
            for k in range(2):
                rows = pl.ds(pl.multiple_of(i * 32 + k * 16, 16), 16)
                place = msg[layer * 4 + 2 + k : layer * 4 + 3 + k, :]
                vcol[rows, :] = jnp.broadcast_to(place, (16, 128))
                count = msg[layer * 4 + k : layer * 4 + k + 1, :]
                ccol[rows, :] = jnp.broadcast_to(count, (16, 128)).astype(BF)

        ramp = lax.broadcasted_iota(jnp.int32, (1024, 128), 0) % 16
        vrow = (vcol[...] + ramp.astype(F32)).T[0:1, :]
        spot = lax.broadcasted_iota(jnp.int32, (256, 1024), 0).astype(F32)
        lhs[layer] = jnp.where(spot == vrow, 1.0, 0.0).astype(BF)
        degree = dot(lhs[layer], ccol[...])
        lane = lax.broadcasted_iota(jnp.int32, (256, 128), 1)
        within = lax.broadcasted_iota(jnp.int32, (256, 128), 0) % 16
        for g in range(8):
            here = jnp.sum(jnp.where(lane == within + g * 16, degree, 0.0), axis=1, keepdims=True)
            rdeg[g] = jnp.broadcast_to(1.0 / jnp.maximum(here, 1.0), (256, 128))

    def piece_copy(phase, i):
        c = phase % 2
        return remote(
            sendbuf[c].at[i], recv[phase].at[i], aa_s.at[phase, i], aa_r.at[phase, i], peer(i)
        )

    def piece(layer, values, c, i, k):
        return dot(maskt[layer, tab[layer, i, k]], values[c][tab[layer, i, 2 + k]]).astype(BF)

    def pieces(phase, values):
        layer, c = phase // 2, phase % 2
        if layer == 1:

            @pl.loop(1, 32)
            def _(i):
                piece_copy(c, i).wait_send()

        @pl.loop(1, 32)
        def _(i):
            for k in range(2):
                sendbuf[c][i, k] = piece(layer, values, c, i, k)
            piece_copy(phase, i).start()

        for k in range(2):
            recv[phase][0, k] = piece(layer, values, c, 0, k)

    def gather_tiles(phase, result):
        layer, c = phase // 2, phase % 2

        @pl.loop(1, 32)
        def _(i):
            piece_copy(phase, i).wait_recv()

        for g in range(8):
            rows = pl.ds(g * 16, 16)
            got = recv[phase][:, :, rows, :].reshape(1024, 128)
            mean = dot(lhs[layer], got) * rdeg[g]
            if layer == 0:
                mean = jnp.maximum(own[2 + c, :, rows, :].reshape(256, 128) + mean, 0.0)
            result[c][:, rows, :] = mean.astype(BF).reshape(16, 16, 128)

    far = (right, left, opp)

    def rows_copies(m, c, values):
        return [
            remote(
                values[c].at[pl.ds(d * 4, 4)], hm[m][c].at[f],
                rows_s.at[m, c, k], rows_r.at[m, c, k], (d, n),
            )
            for k, d in enumerate(far)
        ]

    def rows_send(m, c, values):
        start(rows_copies(m, c, values))
        hm[m][c][f] = values[c][pl.ds(f * 4, 4)]

    def rows_wait(m, c, values):
        for copy in rows_copies(m, c, values):
            copy.wait_recv()

    def cot_copies():
        return [
            remote(
                cot_hbm.at[pl.ds(pl.multiple_of(d * 512, 512), 512)], cot.at[f],
                cot_s.at[k], cot_r.at[k], (d, n),
            )
            for k, d in enumerate(far)
        ]

    back = (left, right, opp)
    chip = z * 4 + y

    def w2_first(k, m=0):
        rows = pl.ds(pl.multiple_of(chip * 16, 16), 16)
        src = (ws2_hbm, wn2_hbm)[m].at[rows]
        return remote(src, wx.at[k], w2_s.at[k], w2_r.at[k], (far[k], n))

    def w2_place(k):
        return w2.at[core, back[k], pl.ds(pl.multiple_of(chip * 16, 16), 16)]

    def w2_spread(i, k):
        zz = (z + sign * (i // 4) + 4) % 4
        yy = (y + sign * (i % 4) + 4) % 4
        dev = (f, zz * 8 + yy * 2 + core)
        return remote(wx.at[k], w2_place(k), ws_s.at[i, k], ws_r.at[i, k], dev)

    def w2_forward(d, k):
        return remote(
            w2.at[core, d], w2.at[core, d], wd_s.at[k], wd_r.at[k], (f, other)
        )

    def pre_add(m, c, first):
        left_side = jnp.concatenate([hm[m][c][s].reshape(512, 128) for s in range(4)], axis=1)

        @pl.loop(0, 4)
        def _(j):
            cols = pl.ds(pl.multiple_of(j * 256, 256), 256)
            part = dot(left_side, w2[m, :, c * 128 : (c + 1) * 128, cols].reshape(512, 256))
            for half in range(2):
                new = part[:, half * 128 : (half + 1) * 128].reshape(4, 128, 128)
                at = pl.ds(j * 4, 4)
                own[half, at] = new if first else own[half, at] + new

    def x_copy(c, m=0):
        return remote(hm[m][c], xoth[c], x_s.at[c], x_r.at[c], (f, other))

    def x_send(c):
        for m in range(2):

            @pl.when(core == 1 - m)
            def _():
                x_copy(c, m).start()

    def transpose_x(c):
        for m in range(2):

            @pl.when(core == m)
            def _():
                for s in range(4):
                    mine = hm[m][c][s].reshape(512, 128).astype(F32).T.astype(BF)
                    xt[c, s * 128 : (s + 1) * 128, 0:512] = mine

        x_copy(c).wait_recv()
        for s in range(4):
            theirs = xoth[c][s].reshape(512, 128).astype(F32).T.astype(BF)
            xt[c, s * 128 : (s + 1) * 128, 512:1024] = theirs

    def slope_copy():
        return remote(slope_own, slope_oth, sl_s.at[0], sl_r.at[0], (f, other))

    def h2_copies():
        return [
            remote(
                feat.at[pl.ds(pl.multiple_of(d * 512, 512), 512), pl.ds(0, 256)], hid2_out.at[pl.ds(pl.multiple_of(f * 512, 512), 512)],
                h2_s.at[k], h2_r.at[k], (d, n),
            )
            for k, d in enumerate(far)
        ]

    def along_y(d):
        return (f, z * 8 + ((y + d) % 4) * 2 + core)

    def along_z(d):
        return (f, ((z + d) % 4) * 8 + y * 2 + core)

    def g1_copies(h):
        out = []
        for d in (1, 2, 3):
            if h == 0:
                src, dev = g0.at[:, :, (y + d) % 4], along_y(d)
            else:
                src, dev = g1.at[:, (z + d) % 4], along_z(d)
            out.append(remote(src, r1[h].at[d - 1], g1_s.at[h, d - 1], g1_r.at[h, d - 1], dev))
        return out

    def g2_copies(h):
        out = []
        for d in (1, 2, 3):
            to = (z + d) % 4 if h == 0 else (y + d) % 4
            dev = along_z(d) if h == 0 else along_y(d)
            out.append(remote(s1[h].at[:, to], r2[h].at[d - 1], g2_s.at[h, d - 1], g2_r.at[h, d - 1], dev))
        return out

    def g3_copies(h):
        return [
            remote(
                s2[h].at[(f + d) % 4], r3[h].at[d - 1],
                g3_s.at[h, d - 1], g3_r.at[h, d - 1], ((f + d) % 4, n),
            )
            for d in (1, 2, 3)
        ]

    def fin_copy():
        rows = pl.ds(pl.multiple_of((1 - core) * 8, 8), 8)
        return remote(fin.at[rows], finr, fn_s.at[0], fn_r.at[0], (f, other))

    for m in range(2):

        @pl.when(core == m)
        def _():
            for k in range(3):
                w2_first(k, m).start()

    loads[0].wait()
    loads[1].wait()
    project(NEIGH, opp, 0)
    start(copies_a(0))
    project(NEIGH, right, 1)
    project(NEIGH, left, 2)
    start(copies_direct(0))
    project(NEIGH, f, None)
    for c in loads[2:]:
        c.wait()
    for k in range(3):
        w2_first(k).wait_recv()

    @pl.loop(1, 16)
    def _(i):
        for k in range(3):
            w2_spread(i, k).start()

    for k in range(3):
        local(wx.at[k], w2_place(k), 10 + k).start()
    ring_add(0)
    start(copies_a(1))
    start(copies_direct(1))
    masks_of(0, mask1)
    slots_of(0, src1)
    project(SELF, opp, 0)
    project(SELF, right, 1)
    project(SELF, left, 2)
    ring_end(0)
    pieces(0, proj)
    ring_add(1)
    start(copies_a(2))
    start(copies_direct(2))
    project(SELF, f, None)
    load_mask2.wait()
    masks_of(1, mask2)
    slots_of(1, src2)
    meta_send()
    start(copies_a(3))
    ring_end(1)
    pieces(1, proj)
    ring_add(2)
    start(copies_direct(3))
    meta_wait()
    build(0)
    ring_add(3)

    @pl.loop(1, 16)
    def _(i):
        for k in range(3):
            w2_spread(i, k).wait_recv()

    for k in range(3):
        local(wx.at[k], w2_place(k), 10 + k).wait()
    for k, d in enumerate(far):
        w2_forward(d, k).start()
    ring_end(2)
    gather_tiles(0, hid)
    pieces(2, hid)
    rows_send(0, 0, hid)
    start(cot_copies())
    ring_end(3)
    gather_tiles(1, hid)
    pieces(3, hid)
    rows_send(0, 1, hid)
    build(1)
    rows_wait(0, 0, hid)
    rows_wait(0, 1, hid)
    for k, d in enumerate(far):
        w2_forward(d, k).wait_recv()
    pre_add(0, 0, True)
    pre_add(0, 1, False)
    gather_tiles(2, proj)
    rows_send(1, 0, proj)
    rows_wait(1, 0, proj)
    x_send(0)
    pre_add(1, 0, False)
    transpose_x(0)
    gather_tiles(3, proj)
    rows_send(1, 1, proj)
    for c in cot_copies():
        c.wait_recv()
    rows_wait(1, 1, proj)
    x_send(1)
    pre_add(1, 1, False)
    for j in range(4):

        @pl.loop(0, 4)
        def _(t):
            rows = pl.ds(pl.multiple_of(t * 128, 128), 128)
            out_rows = pl.ds(pl.multiple_of(t * 128 + j * 512, 128), 128)
            for half in range(2):
                cols = slice(half * 128, (half + 1) * 128)
                v = own[half, j * 4 + t]
                s = 1.0 / (1.0 + jnp.exp(-v))
                feat[out_rows, cols] = (v * s).astype(BF)
                up = cot[j, rows, cols].astype(F32) * s * (1.0 + v * (1.0 - s))
                slope_own[j, rows, cols] = up.astype(BF)

    slope_copy().start()
    start(h2_copies())
    mine = pl.ds(pl.multiple_of(f * 512, 512), 512)
    hid2_out[mine, :] = feat[mine, 0:256]
    transpose_x(1)
    slope_copy().wait_recv()
    for j in range(4):
        up = jnp.concatenate([slope_own[j], slope_oth[j]], axis=0)
        grad = g0 if j < 2 else g1
        cols = pl.ds((j % 2) * 256, 256)
        for c in range(2):
            part = dot(xt[c], up).astype(BF)
            grad[:, 2 * c : 2 * c + 2, :, :, cols] = part.reshape(4, 2, 4, 16, 256)
        if j == 1:
            start(g1_copies(0))
        if j == 3:
            start(g1_copies(1))
    for h in range(2):
        for c in g1_copies(h):
            c.wait_recv()
        first = g0[:, :, y] if h == 0 else g1[:, z]
        total = first.astype(F32)
        for d in range(3):
            total = total + r1[h][d].astype(F32)
        s1[h][...] = total
        start(g2_copies(h))
    for h in range(2):
        for c in g2_copies(h):
            c.wait_recv()
        at = z if h == 0 else y
        s2[h][...] = s1[h][:, at] + r2[h][0] + r2[h][1] + r2[h][2]
        start(g3_copies(h))
    for h in range(2):
        for c in g3_copies(h):
            c.wait_recv()
        fin[:, h * 512 : (h + 1) * 512] = s2[h][f] + r3[h][0] + r3[h][1] + r3[h][2]
    fin_copy().start()
    fin_copy().wait_recv()
    mine8 = fin[pl.ds(pl.multiple_of(core * 8, 8), 8), :]
    first_core = jnp.full((8, 1024), core, jnp.int32) == 0
    gs_out[...] = jnp.where(first_core, mine8, finr[...])
    gn_out[...] = jnp.where(first_core, finr[...], mine8)

    for c in h2_copies():
        c.wait_recv()
    for q in range(4):
        for c in copies_a(q) + copies_direct(q) + copies_added(q):
            c.wait_send()

    @pl.loop(1, 16)
    def _(i):
        for k in range(3):
            w2_spread(i, k).wait_send()

    @pl.loop(1, 32)
    def _(i):
        piece_copy(2, i).wait_send()
        piece_copy(3, i).wait_send()

    for m, values in ((0, hid), (1, proj)):
        for c in range(2):
            for copy in rows_copies(m, c, values):
                copy.wait_send()
    rest = cot_copies() + h2_copies() + [slope_copy(), fin_copy(), x_copy(0), x_copy(1)]
    for k, d in enumerate(far):
        rest += [w2_first(k), w2_forward(d, k)]
    for h in range(2):
        rest += g1_copies(h) + g2_copies(h) + g3_copies(h)
    for copy in rest:
        copy.wait_send()


def local_step(
    features, self_w1, neigh_w1, self_w2, neigh_w2, source_tiles1, owner_blocks1, target_tiles1,
    tile_masks1, source_tiles2, owner_blocks2, target_tiles2, tile_masks2, cotangent,
):
    hbm = pl.BlockSpec(memory_space=pl.ANY)
    smem = pl.BlockSpec(memory_space=pltpu.SMEM)
    vmem = pl.BlockSpec(memory_space=pltpu.VMEM)
    v = pltpu.VMEM
    dma = pltpu.SemaphoreType.DMA

    def pair(*shape):
        return [dma(shape), dma(shape)]

    i32 = jnp.int32
    scratch = [
        v((2048, 512), BF), *[v((512, 1024), BF)] * 2, *[v((32, 128, 128), i32)] * 2,
        v((2, 32, 128, 128), BF), v((2, 32, 8, 128), F32), pltpu.SMEM((2, 32, 8), i32),
        *[v((3, 2048, 128), BF)] * 4, v((4, 16, 128, 128), F32), *[v((2, 1024, 128), BF)] * 4,
        *[v((2, 2048, 128), BF)] * 4, *[v((16, 128, 128), BF)] * 4,
        v((32, 8, 128), F32), v((32, 8, 128), F32), v((1024, 128), F32), v((1024, 128), BF),
        v((2, 256, 1024), BF), v((8, 256, 128), F32),
        *[v((32, 2, 128, 128), BF)] * 6, *[v((4, 4, 128, 128), BF)] * 6, v((2, 512, 1024), BF),
        v((4, 512, 256), BF), v((2, 4, 256, 1024), BF), v((3, 16, 1024), BF), *[v((4, 512, 256), BF)] * 2,
        *[v((4, 4, 4, 16, 512), BF)] * 2, *[v((3, 4, 4, 16, 512), BF)] * 2,
        *[v((4, 4, 16, 512), F32)] * 2, *[v((3, 4, 16, 512), F32)] * 2, *[v((4, 16, 512), F32)] * 2,
        *[v((3, 16, 512), F32)] * 2, v((16, 1024), F32), v((8, 1024), F32),
        dma((13,)),
        *pair(32), *pair(4, 2), *pair(4, 4), *pair(4, 32), *pair(2, 2, 3), *pair(3), *pair(3),
        *pair(16, 3), *pair(3), *pair(2), *pair(1), *pair(3), *pair(2, 3), *pair(2, 3), *pair(2, 3), *pair(1),
    ]
    hidden2, grad_self, grad_neigh = pl.pallas_call(
        kernel,
        out_shape=(
            jax.ShapeDtypeStruct((2048, 256), BF),
            jax.ShapeDtypeStruct((8, 1024), F32),
            jax.ShapeDtypeStruct((8, 1024), F32),
        ),
        in_specs=[hbm] * 5 + [smem] * 2 + [hbm] + [smem] * 2 + [hbm, smem, hbm],
        out_specs=(vmem, vmem, vmem),
        scratch_shapes=scratch,
        compiler_params=pltpu.CompilerParams(
            collective_id=0, has_side_effects=True, vmem_limit_bytes=(64 << 20) - (64 << 10)
        ),
        cost_estimate=pl.CostEstimate(flops=10**10, bytes_accessed=16 << 20, transcendentals=1 << 19),
        name="sage",
    )(
        features, self_w1, neigh_w1, self_w2, neigh_w2, source_tiles1, target_tiles1, tile_masks1,
        source_tiles2, target_tiles2, tile_masks2,
        jnp.concatenate([owner_blocks1[:, 0], owner_blocks2[:, 0]]), cotangent,
    )
    return hidden2, grad_self, grad_neigh


def solution(mesh):
    node3 = P("node", None, None)
    in_specs = (
        P("node", "feat"), P("feat", None), P("feat", None), P("feat", None), P("feat", None),
        P("node"), P("node", None), P("node"), node3,
        P("node"), P("node", None), P("node"), node3, P("node", "feat"),
    )
    out_specs = (P("node", "feat"), P(("feat", "node"), None), P(("feat", "node"), None))
    return jax.shard_map(local_step, mesh=mesh, in_specs=in_specs, out_specs=out_specs, check_vma=False)
```

```python
import functools

import jax
import jax.numpy as jnp
from jax import lax
from jax.experimental import pallas as pl
from jax.experimental.pallas import tpu as pltpu
from jax.sharding import PartitionSpec as P

MESH = pl.DeviceIdType.MESH
BF = jnp.bfloat16
F32 = jnp.float32
NEIGH, SELF = 0, 1


def dot(a, b):
    return jnp.dot(a, b, preferred_element_type=F32)


def kernel(
    feat_hbm, ws1_hbm, wn1_hbm, ws2_hbm, wn2_hbm,
    src1, tgt1, mask1_hbm, src2, tgt2, mask2_hbm, owners, cot_hbm,
    hid2_out, gs_out, gn_out,
    feat, w1n, w1s, mask1, mask2, maskt, cnt, tab,
    p0, p1, p2, p3, own, a0, a1, a2, a3, b0, b1, b2, b3, proj0, proj1, hid0, hid1,
    msg_out, msg_in, vcol, ccol, lhs, rdeg,
    send0, send1, recv0, recv1, recv2, recv3, h0, h1, m0, m1, xoth0, xoth1, xt,
    cot, w2, wx, slope_own, slope_oth,
    g0, g1, r1a, r1b, s1a, s1b, r2a, r2b, s2a, s2b, r3a, r3b, fin, finr,
    ld, meta_s, meta_r, ra_s, ra_r, rb_s, rb_r, aa_s, aa_r, rows_s, rows_r,
    cot_s, cot_r, w2_s, w2_r, ws_s, ws_r, wd_s, wd_r, x_s, x_r, sl_s, sl_r, h2_s, h2_r,
    g1_s, g1_r, g2_s, g2_r, g3_s, g3_r, fn_s, fn_r,
):
    f = lax.axis_index("feat")
    n = lax.axis_index("node")
    z, y, core = n // 8, (n // 2) % 4, n % 2
    sign = 1 - 2 * core
    right, left, opp = (f + 1) % 4, (f + 3) % 4, (f + 2) % 4
    other = n + sign
    proj, hid = (proj0, proj1), (hid0, hid1)
    psend, buf_a, buf_b = (p0, p1, p2, p3), (a0, a1, a2, a3), (b0, b1, b2, b3)
    sendbuf, recv = (send0, send1), (recv0, recv1, recv2, recv3)
    hm, xoth = ((h0, h1), (m0, m1)), (xoth0, xoth1)
    r1, s1, r2, s2, r3 = (r1a, r1b), (s1a, s1b), (r2a, r2b), (s2a, s2b), (r3a, r3b)

    def peer(i):
        j, ii, dc = i // 8, (i // 2) % 4, i % 2
        zz = (z + sign * ii + 4) % 4
        yy = (y + sign * ((ii + j) % 4) + 4) % 4
        return (f, zz * 8 + yy * 2 + (core + dc) % 2)

    def remote(src, dst, ss, rs, dev):
        return pltpu.make_async_remote_copy(
            src_ref=src, dst_ref=dst, send_sem=ss, recv_sem=rs, device_id=dev, device_id_type=MESH
        )

    def local(src, dst, k):
        return pltpu.make_async_copy(src, dst, ld.at[k])

    loads = [
        local(feat_hbm, feat, 0),
        local(wn1_hbm, w1n, 1),
        local(ws1_hbm, w1s, 2),
        local(mask1_hbm, mask1, 3),
        local(cot_hbm.at[pl.ds(pl.multiple_of(f * 512, 512), 512)], cot.at[f], 4),
    ]
    for m, ref in ((0, ws2_hbm), (1, wn2_hbm)):
        loads.append(local(ref, w2.at[m, f], 5 + m))
    load_mask2 = local(mask2_hbm, mask2, 9)
    for c in [*loads, load_mask2]:
        c.start()

    barrier = pltpu.get_barrier_semaphore()

    @pl.loop(1, 32)
    def _(i):
        pl.semaphore_signal(barrier, inc=1, device_id=peer(i), device_id_type=MESH)

    for d in (right, left, opp):
        pl.semaphore_signal(barrier, inc=1, device_id=(d, n), device_id_type=MESH)
    pl.semaphore_wait(barrier, 34)

    def project(mat, j, where):
        cols = pl.ds(pl.multiple_of(j * 256, 256), 256)

        @pl.loop(0, 4)
        def _(t):
            rows = pl.ds(pl.multiple_of(t * 512, 512), 512)
            part = dot(feat[rows, :], (w1n, w1s)[mat][:, cols])
            for c in range(2):
                half = part[:, c * 128 : (c + 1) * 128]
                if where is None:
                    own[2 * mat + c, pl.ds(t * 4, 4)] = half.reshape(4, 128, 128)
                else:
                    psend[2 * mat + c][where, rows, :] = half.astype(BF)

    lo, hi = pl.ds(0, 1024), pl.ds(1024, 1024)

    def copies_a(q):
        return [
            remote(psend[q].at[0, lo], buf_a[q].at[0], ra_s.at[q, 0], ra_r.at[q, 0], (right, n)),
            remote(psend[q].at[0, hi], buf_a[q].at[1], ra_s.at[q, 1], ra_r.at[q, 1], (left, n)),
        ]

    def copies_direct(q):
        return [
            remote(psend[q].at[1, hi], buf_b[q].at[0, hi], rb_s.at[q, 0], rb_r.at[q, 0], (right, n)),
            remote(psend[q].at[2, lo], buf_b[q].at[1, lo], rb_s.at[q, 1], rb_r.at[q, 1], (left, n)),
        ]

    def copies_added(q):
        return [
            remote(psend[q].at[1, lo], buf_b[q].at[0, lo], rb_s.at[q, 2], rb_r.at[q, 2], (right, n)),
            remote(psend[q].at[2, hi], buf_b[q].at[1, hi], rb_s.at[q, 3], rb_r.at[q, 3], (left, n)),
        ]

    def start(copies):
        for c in copies:
            c.start()

    def ring_add(q):
        a, b = copies_a(q), copies_added(q)
        for s, base in ((0, 0), (1, 1024)):
            a[s].wait_recv()

            @pl.loop(0, 4)
            def _(t):
                rows = pl.ds(pl.multiple_of(t * 256 + base, 256), 256)
                from_rows = pl.ds(pl.multiple_of(t * 256, 256), 256)
                total = psend[q][1 + s, rows, :].astype(F32) + buf_a[q][s, from_rows, :].astype(F32)
                psend[q][1 + s, rows, :] = total.astype(BF)

            b[s].start()

    def ring_end(q):
        for c in copies_direct(q) + copies_added(q):
            c.wait_recv()

        @pl.loop(0, 8)
        def _(t):
            rows = pl.ds(pl.multiple_of(t * 256, 256), 256)
            got = buf_b[q][0, rows, :].astype(F32) + buf_b[q][1, rows, :].astype(F32)
            total = own[q, pl.ds(t * 2, 2)] + got.reshape(2, 128, 128)
            if q < 2:
                proj[q][pl.ds(t * 2, 2)] = total.astype(BF)
            else:
                own[q, pl.ds(t * 2, 2)] = total

    def masks_of(layer, mask):
        @pl.loop(0, 32)
        def _(e):
            m = mask[e].astype(F32)
            cnt[layer, e] = jnp.broadcast_to(jnp.sum(m, axis=0, keepdims=True), (8, 128))
            maskt[layer, e] = m.T.astype(BF)

    def slots_of(layer, sources):
        @pl.loop(0, 32)
        def _(i):
            who = peer(i)[1]

            def look(e, carry):
                seen, first, second = carry
                hit = owners[layer * 32 + e] == who
                first = jnp.where(jnp.logical_and(hit, seen == 0), e, first)
                second = jnp.where(jnp.logical_and(hit, seen == 1), e, second)
                return seen + hit.astype(jnp.int32), first, second

            zero = jnp.int32(0)
            seen, first, second = lax.fori_loop(0, 32, look, (zero, zero, zero), unroll=8)
            tab[layer, i, 0] = first
            tab[layer, i, 1] = second
            tab[layer, i, 2] = sources[first]
            tab[layer, i, 3] = sources[second]
            tab[layer, i, 4] = seen

    def meta_copy(i):
        return remote(msg_out.at[i], msg_in.at[i], meta_s.at[i], meta_r.at[i], peer(i))

    def message(i):
        row = lax.broadcasted_iota(jnp.int32, (8, 128), 0)
        msg = jnp.zeros((8, 128), F32)
        for layer, targets in ((0, tgt1), (1, tgt2)):
            for k in range(2):
                e = tab[layer, i, k]
                used = tab[layer, i, 4] > k
                place = jnp.where(used, targets[e] * 16, -1024).astype(F32)
                msg = jnp.where(row == layer * 4 + k, cnt[layer, e], msg)
                msg = jnp.where(row == layer * 4 + 2 + k, place, msg)
        return msg

    def meta_send():
        msg_in[0] = message(0)

        @pl.loop(1, 32)
        def _(i):
            msg_out[i] = message(i)
            meta_copy(i).start()

    def meta_wait():
        @pl.loop(1, 32)
        def _(i):
            meta_copy(i).wait()

    def build(layer):
        @pl.loop(0, 32)
        def _(i):
            msg = msg_in[i]
            for k in range(2):
                rows = pl.ds(pl.multiple_of(i * 32 + k * 16, 16), 16)
                place = msg[layer * 4 + 2 + k : layer * 4 + 3 + k, :]
                vcol[rows, :] = jnp.broadcast_to(place, (16, 128))
                count = msg[layer * 4 + k : layer * 4 + k + 1, :]
                ccol[rows, :] = jnp.broadcast_to(count, (16, 128)).astype(BF)

        ramp = lax.broadcasted_iota(jnp.int32, (1024, 128), 0) % 16
        vrow = (vcol[...] + ramp.astype(F32)).T[0:1, :]
        spot = lax.broadcasted_iota(jnp.int32, (256, 1024), 0).astype(F32)
        lhs[layer] = jnp.where(spot == vrow, 1.0, 0.0).astype(BF)
        degree = dot(lhs[layer], ccol[...])
        lane = lax.broadcasted_iota(jnp.int32, (256, 128), 1)
        within = lax.broadcasted_iota(jnp.int32, (256, 128), 0) % 16
        for g in range(8):
            here = jnp.sum(jnp.where(lane == within + g * 16, degree, 0.0), axis=1, keepdims=True)
            rdeg[g] = jnp.broadcast_to(1.0 / jnp.maximum(here, 1.0), (256, 128))

    def piece_copy(phase, i):
        c = phase % 2
        return remote(
            sendbuf[c].at[i], recv[phase].at[i], aa_s.at[phase, i], aa_r.at[phase, i], peer(i)
        )

    def piece(layer, values, c, i, k):
        return dot(maskt[layer, tab[layer, i, k]], values[c][tab[layer, i, 2 + k]]).astype(BF)

    def pieces(phase, values):
        layer, c = phase // 2, phase % 2
        if layer == 1:

            @pl.loop(1, 32)
            def _(i):
                piece_copy(c, i).wait_send()

        @pl.loop(1, 32)
        def _(i):
            for k in range(2):
                sendbuf[c][i, k] = piece(layer, values, c, i, k)
            piece_copy(phase, i).start()

        for k in range(2):
            recv[phase][0, k] = piece(layer, values, c, 0, k)

    def gather_tiles(phase, result):
        layer, c = phase // 2, phase % 2

        @pl.loop(1, 32)
        def _(i):
            piece_copy(phase, i).wait_recv()

        for g in range(8):
            rows = pl.ds(g * 16, 16)
            got = recv[phase][:, :, rows, :].reshape(1024, 128)
            mean = dot(lhs[layer], got) * rdeg[g]
            if layer == 0:
                mean = jnp.maximum(own[2 + c, :, rows, :].reshape(256, 128) + mean, 0.0)
            result[c][:, rows, :] = mean.astype(BF).reshape(16, 16, 128)

    far = (right, left, opp)

    def rows_copies(m, c, values):
        return [
            remote(
                values[c].at[pl.ds(d * 4, 4)], hm[m][c].at[f],
                rows_s.at[m, c, k], rows_r.at[m, c, k], (d, n),
            )
            for k, d in enumerate(far)
        ]

    def rows_send(m, c, values):
        start(rows_copies(m, c, values))
        hm[m][c][f] = values[c][pl.ds(f * 4, 4)]

    def rows_wait(m, c, values):
        for copy in rows_copies(m, c, values):
            copy.wait_recv()

    def cot_copies():
        return [
            remote(
                cot_hbm.at[pl.ds(pl.multiple_of(d * 512, 512), 512)], cot.at[f],
                cot_s.at[k], cot_r.at[k], (d, n),
            )
            for k, d in enumerate(far)
        ]

    chip = z * 4 + y
    slice_rows = pl.ds(pl.multiple_of(chip * 16, 16), 16)

    def w2_near(k):
        return remote(w2.at[core, f], w2.at[core, f], w2_s.at[k], w2_r.at[k], (far[k], n))

    def w2_first(m=0):
        src = (ws2_hbm, wn2_hbm)[m].at[slice_rows]
        return remote(src, wx, w2_s.at[2], w2_r.at[2], (opp, n))

    def w2_own():
        return local(wx, w2.at[core, opp, slice_rows], 10)

    def w2_spread(i):
        zz = (z + sign * (i // 4) + 4) % 4
        yy = (y + sign * (i % 4) + 4) % 4
        dev = (f, zz * 8 + yy * 2 + core)
        return remote(wx, w2.at[core, opp, slice_rows], ws_s.at[i], ws_r.at[i], dev)

    def w2_forward(d, k):
        return remote(
            w2.at[core, d], w2.at[core, d], wd_s.at[k], wd_r.at[k], (f, other)
        )

    def pre_add(m, c, first):
        left_side = jnp.concatenate([hm[m][c][s].reshape(512, 128) for s in range(4)], axis=1)

        @pl.loop(0, 4)
        def _(j):
            cols = pl.ds(pl.multiple_of(j * 256, 256), 256)
            part = dot(left_side, w2[m, :, c * 128 : (c + 1) * 128, cols].reshape(512, 256))
            for half in range(2):
                new = part[:, half * 128 : (half + 1) * 128].reshape(4, 128, 128)
                at = pl.ds(j * 4, 4)
                own[half, at] = new if first else own[half, at] + new

    def x_copy(c, m=0):
        return remote(hm[m][c], xoth[c], x_s.at[c], x_r.at[c], (f, other))

    def x_send(c):
        for m in range(2):

            @pl.when(core == 1 - m)
            def _():
                x_copy(c, m).start()

    def transpose_x(c):
        for m in range(2):

            @pl.when(core == m)
            def _():
                for s in range(4):
                    mine = hm[m][c][s].reshape(512, 128).astype(F32).T.astype(BF)
                    xt[c, s * 128 : (s + 1) * 128, 0:512] = mine

        x_copy(c).wait_recv()
        for s in range(4):
            theirs = xoth[c][s].reshape(512, 128).astype(F32).T.astype(BF)
            xt[c, s * 128 : (s + 1) * 128, 512:1024] = theirs

    def slope_copy():
        return remote(slope_own, slope_oth, sl_s.at[0], sl_r.at[0], (f, other))

    def h2_copies():
        return [
            remote(
                feat.at[pl.ds(pl.multiple_of(d * 512, 512), 512), pl.ds(0, 256)], hid2_out.at[pl.ds(pl.multiple_of(f * 512, 512), 512)],
                h2_s.at[k], h2_r.at[k], (d, n),
            )
            for k, d in enumerate(far)
        ]

    def along_y(d):
        return (f, z * 8 + ((y + d) % 4) * 2 + core)

    def along_z(d):
        return (f, ((z + d) % 4) * 8 + y * 2 + core)

    def g1_copies(h):
        out = []
        for d in (1, 2, 3):
            if h == 0:
                src, dev = g0.at[:, :, (y + d) % 4], along_y(d)
            else:
                src, dev = g1.at[:, (z + d) % 4], along_z(d)
            out.append(remote(src, r1[h].at[d - 1], g1_s.at[h, d - 1], g1_r.at[h, d - 1], dev))
        return out

    def g2_copies(h):
        out = []
        for d in (1, 2, 3):
            to = (z + d) % 4 if h == 0 else (y + d) % 4
            dev = along_z(d) if h == 0 else along_y(d)
            out.append(remote(s1[h].at[:, to], r2[h].at[d - 1], g2_s.at[h, d - 1], g2_r.at[h, d - 1], dev))
        return out

    def g3_copies(h):
        return [
            remote(
                s2[h].at[(f + d) % 4], r3[h].at[d - 1],
                g3_s.at[h, d - 1], g3_r.at[h, d - 1], ((f + d) % 4, n),
            )
            for d in (1, 2, 3)
        ]

    def fin_copy():
        rows = pl.ds(pl.multiple_of((1 - core) * 8, 8), 8)
        return remote(fin.at[rows], finr, fn_s.at[0], fn_r.at[0], (f, other))

    for m in range(2):

        @pl.when(core == m)
        def _():
            w2_first(m).start()

    loads[0].wait()
    loads[1].wait()
    project(NEIGH, opp, 0)
    start(copies_a(0))
    project(NEIGH, right, 1)
    project(NEIGH, left, 2)
    start(copies_direct(0))
    project(NEIGH, f, None)
    for c in loads[2:]:
        c.wait()
    w2_first().wait_recv()

    @pl.loop(1, 16)
    def _(i):
        w2_spread(i).start()

    w2_own().start()
    ring_add(0)
    start(copies_a(1))
    start(copies_direct(1))
    masks_of(0, mask1)
    slots_of(0, src1)
    project(SELF, opp, 0)
    project(SELF, right, 1)
    project(SELF, left, 2)
    ring_end(0)
    pieces(0, proj)
    ring_add(1)
    start(copies_a(2))
    start(copies_direct(2))
    project(SELF, f, None)
    load_mask2.wait()
    masks_of(1, mask2)
    slots_of(1, src2)
    meta_send()
    start(copies_a(3))
    ring_end(1)
    pieces(1, proj)
    ring_add(2)
    start(copies_direct(3))
    meta_wait()
    build(0)
    ring_add(3)

    for k in range(2):
        w2_near(k).start()
    ring_end(2)
    gather_tiles(0, hid)
    pieces(2, hid)
    rows_send(0, 0, hid)
    start(cot_copies())
    ring_end(3)
    gather_tiles(1, hid)
    pieces(3, hid)
    rows_send(0, 1, hid)
    w2_own().wait()

    @pl.loop(1, 16)
    def _(i):
        w2_spread(i).wait_recv()

    build(1)
    for k in range(2):
        w2_near(k).wait_recv()
    for k, d in enumerate(far):
        w2_forward(d, k).start()
    rows_wait(0, 0, hid)
    rows_wait(0, 1, hid)
    for k, d in enumerate(far):
        w2_forward(d, k).wait_recv()
    pre_add(0, 0, True)
    pre_add(0, 1, False)
    gather_tiles(2, proj)
    rows_send(1, 0, proj)
    rows_wait(1, 0, proj)
    x_send(0)
    pre_add(1, 0, False)
    transpose_x(0)
    gather_tiles(3, proj)
    rows_send(1, 1, proj)
    for c in cot_copies():
        c.wait_recv()
    rows_wait(1, 1, proj)
    x_send(1)
    pre_add(1, 1, False)
    for j in range(4):

        @pl.loop(0, 4)
        def _(t):
            rows = pl.ds(pl.multiple_of(t * 128, 128), 128)
            out_rows = pl.ds(pl.multiple_of(t * 128 + j * 512, 128), 128)
            for half in range(2):
                cols = slice(half * 128, (half + 1) * 128)
                v = own[half, j * 4 + t]
                s = 1.0 / (1.0 + jnp.exp(-v))
                feat[out_rows, cols] = (v * s).astype(BF)
                up = cot[j, rows, cols].astype(F32) * s * (1.0 + v * (1.0 - s))
                slope_own[j, rows, cols] = up.astype(BF)

    slope_copy().start()
    start(h2_copies())
    mine = pl.ds(pl.multiple_of(f * 512, 512), 512)
    hid2_out[mine, :] = feat[mine, 0:256]
    transpose_x(1)
    slope_copy().wait_recv()
    for j in range(4):
        up = jnp.concatenate([slope_own[j], slope_oth[j]], axis=0)
        grad = g0 if j < 2 else g1
        cols = pl.ds((j % 2) * 256, 256)
        for c in range(2):
            part = dot(xt[c], up).astype(BF)
            grad[:, 2 * c : 2 * c + 2, :, :, cols] = part.reshape(4, 2, 4, 16, 256)
        if j == 1:
            start(g1_copies(0))
        if j == 3:
            start(g1_copies(1))
    for h in range(2):
        for c in g1_copies(h):
            c.wait_recv()
        first = g0[:, :, y] if h == 0 else g1[:, z]
        total = first.astype(F32)
        for d in range(3):
            total = total + r1[h][d].astype(F32)
        s1[h][...] = total
        start(g2_copies(h))
    for h in range(2):
        for c in g2_copies(h):
            c.wait_recv()
        at = z if h == 0 else y
        s2[h][...] = s1[h][:, at] + r2[h][0] + r2[h][1] + r2[h][2]
        start(g3_copies(h))
    for h in range(2):
        for c in g3_copies(h):
            c.wait_recv()
        fin[:, h * 512 : (h + 1) * 512] = s2[h][f] + r3[h][0] + r3[h][1] + r3[h][2]
    fin_copy().start()
    fin_copy().wait_recv()
    mine8 = fin[pl.ds(pl.multiple_of(core * 8, 8), 8), :]
    first_core = jnp.full((8, 1024), core, jnp.int32) == 0
    gs_out[...] = jnp.where(first_core, mine8, finr[...])
    gn_out[...] = jnp.where(first_core, finr[...], mine8)

    for c in h2_copies():
        c.wait_recv()
    for q in range(4):
        for c in copies_a(q) + copies_direct(q) + copies_added(q):
            c.wait_send()

    @pl.loop(1, 16)
    def _(i):
        w2_spread(i).wait_send()

    @pl.loop(1, 32)
    def _(i):
        piece_copy(2, i).wait_send()
        piece_copy(3, i).wait_send()

    for m, values in ((0, hid), (1, proj)):
        for c in range(2):
            for copy in rows_copies(m, c, values):
                copy.wait_send()
    rest = cot_copies() + h2_copies() + [slope_copy(), fin_copy(), x_copy(0), x_copy(1)]
    rest += [w2_near(0), w2_near(1), w2_first()] + [w2_forward(d, k) for k, d in enumerate(far)]
    for h in range(2):
        rest += g1_copies(h) + g2_copies(h) + g3_copies(h)
    for copy in rest:
        copy.wait_send()


def local_step(
    features, self_w1, neigh_w1, self_w2, neigh_w2, source_tiles1, owner_blocks1, target_tiles1,
    tile_masks1, source_tiles2, owner_blocks2, target_tiles2, tile_masks2, cotangent,
):
    hbm = pl.BlockSpec(memory_space=pl.ANY)
    smem = pl.BlockSpec(memory_space=pltpu.SMEM)
    vmem = pl.BlockSpec(memory_space=pltpu.VMEM)
    v = pltpu.VMEM
    dma = pltpu.SemaphoreType.DMA

    def pair(*shape):
        return [dma(shape), dma(shape)]

    i32 = jnp.int32
    scratch = [
        v((2048, 512), BF), *[v((512, 1024), BF)] * 2, *[v((32, 128, 128), i32)] * 2,
        v((2, 32, 128, 128), BF), v((2, 32, 8, 128), F32), pltpu.SMEM((2, 32, 8), i32),
        *[v((3, 2048, 128), BF)] * 4, v((4, 16, 128, 128), F32), *[v((2, 1024, 128), BF)] * 4,
        *[v((2, 2048, 128), BF)] * 4, *[v((16, 128, 128), BF)] * 4,
        v((32, 8, 128), F32), v((32, 8, 128), F32), v((1024, 128), F32), v((1024, 128), BF),
        v((2, 256, 1024), BF), v((8, 256, 128), F32),
        *[v((32, 2, 128, 128), BF)] * 6, *[v((4, 4, 128, 128), BF)] * 6, v((2, 512, 1024), BF),
        v((4, 512, 256), BF), v((2, 4, 256, 1024), BF), v((16, 1024), BF), *[v((4, 512, 256), BF)] * 2,
        *[v((4, 4, 4, 16, 512), BF)] * 2, *[v((3, 4, 4, 16, 512), BF)] * 2,
        *[v((4, 4, 16, 512), F32)] * 2, *[v((3, 4, 16, 512), F32)] * 2, *[v((4, 16, 512), F32)] * 2,
        *[v((3, 16, 512), F32)] * 2, v((16, 1024), F32), v((8, 1024), F32),
        dma((11,)),
        *pair(32), *pair(4, 2), *pair(4, 4), *pair(4, 32), *pair(2, 2, 3), *pair(3), *pair(3),
        *pair(16), *pair(3), *pair(2), *pair(1), *pair(3), *pair(2, 3), *pair(2, 3), *pair(2, 3), *pair(1),
    ]
    hidden2, grad_self, grad_neigh = pl.pallas_call(
        kernel,
        out_shape=(
            jax.ShapeDtypeStruct((2048, 256), BF),
            jax.ShapeDtypeStruct((8, 1024), F32),
            jax.ShapeDtypeStruct((8, 1024), F32),
        ),
        in_specs=[hbm] * 5 + [smem] * 2 + [hbm] + [smem] * 2 + [hbm, smem, hbm],
        out_specs=(vmem, vmem, vmem),
        scratch_shapes=scratch,
        compiler_params=pltpu.CompilerParams(
            collective_id=0, has_side_effects=True, vmem_limit_bytes=(64 << 20) - (64 << 10)
        ),
        cost_estimate=pl.CostEstimate(flops=10**10, bytes_accessed=16 << 20, transcendentals=1 << 19),
        name="sage",
    )(
        features, self_w1, neigh_w1, self_w2, neigh_w2, source_tiles1, target_tiles1, tile_masks1,
        source_tiles2, target_tiles2, tile_masks2,
        jnp.concatenate([owner_blocks1[:, 0], owner_blocks2[:, 0]]), cotangent,
    )
    return hidden2, grad_self, grad_neigh


def solution(mesh):
    node3 = P("node", None, None)
    in_specs = (
        P("node", "feat"), P("feat", None), P("feat", None), P("feat", None), P("feat", None),
        P("node"), P("node", None), P("node"), node3,
        P("node"), P("node", None), P("node"), node3, P("node", "feat"),
    )
    out_specs = (P("node", "feat"), P(("feat", "node"), None), P(("feat", "node"), None))
    return jax.shard_map(local_step, mesh=mesh, in_specs=in_specs, out_specs=out_specs, check_vma=False)
```

```python
import functools

import jax
import jax.numpy as jnp
from jax import lax
from jax.experimental import pallas as pl
from jax.experimental.pallas import tpu as pltpu
from jax.sharding import PartitionSpec as P

MESH = pl.DeviceIdType.MESH
BF = jnp.bfloat16
F32 = jnp.float32
NEIGH, SELF = 0, 1


def dot(a, b):
    return jnp.dot(a, b, preferred_element_type=F32)


def kernel(
    feat_hbm, ws1_hbm, wn1_hbm, ws2_hbm, wn2_hbm,
    src1, tgt1, mask1_hbm, src2, tgt2, mask2_hbm, owners, cot_hbm,
    hid2_out, gs_out, gn_out,
    feat, w1n, w1s, mask1, mask2, maskt, cnt, tab,
    p0, p1, p2, p3, own, a0, a1, a2, a3, b0, b1, b2, b3, proj0, proj1, hid0, hid1,
    msg_out, msg_in, vcol, ccol, lhs, rdeg,
    send0, send1, recv0, recv1, recv2, recv3, h0, h1, m0, m1, xoth0, xoth1, xt,
    cot, w2, wx, slope_own, slope_oth,
    g0, g1, r1a, r1b, s1a, s1b, r2a, r2b, s2a, s2b, r3a, r3b, fin, finr,
    ld, meta_s, meta_r, ra_s, ra_r, rb_s, rb_r, aa_s, aa_r, rows_s, rows_r,
    cot_s, cot_r, w2_s, w2_r, ws_s, ws_r, wd_s, wd_r, x_s, x_r, sl_s, sl_r, h2_s, h2_r,
    g1_s, g1_r, g2_s, g2_r, g3_s, g3_r, fn_s, fn_r,
):
    f = lax.axis_index("feat")
    n = lax.axis_index("node")
    z, y, core = n // 8, (n // 2) % 4, n % 2
    sign = 1 - 2 * core
    right, left, opp = (f + 1) % 4, (f + 3) % 4, (f + 2) % 4
    other = n + sign
    proj, hid = (proj0, proj1), (hid0, hid1)
    psend, buf_a, buf_b = (p0, p1, p2, p3), (a0, a1, a2, a3), (b0, b1, b2, b3)
    sendbuf, recv = (send0, send1), (recv0, recv1, recv2, recv3)
    hm, xoth = ((h0, h1), (m0, m1)), (xoth0, xoth1)
    r1, s1, r2, s2, r3 = (r1a, r1b), (s1a, s1b), (r2a, r2b), (s2a, s2b), (r3a, r3b)

    def peer(i):
        j, ii, dc = i // 8, (i // 2) % 4, i % 2
        zz = (z + sign * ii + 4) % 4
        yy = (y + sign * ((ii + j) % 4) + 4) % 4
        return (f, zz * 8 + yy * 2 + (core + dc) % 2)

    def remote(src, dst, ss, rs, dev):
        return pltpu.make_async_remote_copy(
            src_ref=src, dst_ref=dst, send_sem=ss, recv_sem=rs, device_id=dev, device_id_type=MESH
        )

    def local(src, dst, k):
        return pltpu.make_async_copy(src, dst, ld.at[k])

    loads = [
        local(feat_hbm, feat, 0),
        local(wn1_hbm, w1n, 1),
        local(ws1_hbm, w1s, 2),
        local(mask1_hbm, mask1, 3),
        local(cot_hbm.at[pl.ds(pl.multiple_of(f * 512, 512), 512)], cot.at[f], 4),
    ]
    for m, ref in ((0, ws2_hbm), (1, wn2_hbm)):
        loads.append(local(ref, w2.at[m, f], 5 + m))
    load_mask2 = local(mask2_hbm, mask2, 9)
    for c in [*loads, load_mask2]:
        c.start()

    barrier = pltpu.get_barrier_semaphore()

    @pl.loop(1, 32)
    def _(i):
        pl.semaphore_signal(barrier, inc=1, device_id=peer(i), device_id_type=MESH)

    for d in (right, left, opp):
        pl.semaphore_signal(barrier, inc=1, device_id=(d, n), device_id_type=MESH)
    pl.semaphore_wait(barrier, 34)

    def project(mat, j, where):
        cols = pl.ds(pl.multiple_of(j * 256, 256), 256)

        @pl.loop(0, 4)
        def _(t):
            rows = pl.ds(pl.multiple_of(t * 512, 512), 512)
            part = dot(feat[rows, :], (w1n, w1s)[mat][:, cols])
            for c in range(2):
                half = part[:, c * 128 : (c + 1) * 128]
                if where is None:
                    own[2 * mat + c, pl.ds(t * 4, 4)] = half.reshape(4, 128, 128)
                else:
                    psend[2 * mat + c][where, rows, :] = half.astype(BF)

    lo, hi = pl.ds(0, 1024), pl.ds(1024, 1024)

    def copies_a(q):
        return [
            remote(psend[q].at[0, lo], buf_a[q].at[0], ra_s.at[q, 0], ra_r.at[q, 0], (right, n)),
            remote(psend[q].at[0, hi], buf_a[q].at[1], ra_s.at[q, 1], ra_r.at[q, 1], (left, n)),
        ]

    def copies_direct(q):
        return [
            remote(psend[q].at[1, hi], buf_b[q].at[0, hi], rb_s.at[q, 0], rb_r.at[q, 0], (right, n)),
            remote(psend[q].at[2, lo], buf_b[q].at[1, lo], rb_s.at[q, 1], rb_r.at[q, 1], (left, n)),
        ]

    def copies_added(q):
        return [
            remote(psend[q].at[1, lo], buf_b[q].at[0, lo], rb_s.at[q, 2], rb_r.at[q, 2], (right, n)),
            remote(psend[q].at[2, hi], buf_b[q].at[1, hi], rb_s.at[q, 3], rb_r.at[q, 3], (left, n)),
        ]

    def start(copies):
        for c in copies:
            c.start()

    def ring_add(q):
        a, b = copies_a(q), copies_added(q)
        for s, base in ((0, 0), (1, 1024)):
            a[s].wait_recv()

            @pl.loop(0, 4)
            def _(t):
                rows = pl.ds(pl.multiple_of(t * 256 + base, 256), 256)
                from_rows = pl.ds(pl.multiple_of(t * 256, 256), 256)
                total = psend[q][1 + s, rows, :].astype(F32) + buf_a[q][s, from_rows, :].astype(F32)
                psend[q][1 + s, rows, :] = total.astype(BF)

            b[s].start()

    def ring_end(q):
        for c in copies_direct(q) + copies_added(q):
            c.wait_recv()

        @pl.loop(0, 8)
        def _(t):
            rows = pl.ds(pl.multiple_of(t * 256, 256), 256)
            got = buf_b[q][0, rows, :].astype(F32) + buf_b[q][1, rows, :].astype(F32)
            total = own[q, pl.ds(t * 2, 2)] + got.reshape(2, 128, 128)
            if q < 2:
                proj[q][pl.ds(t * 2, 2)] = total.astype(BF)
            else:
                own[q, pl.ds(t * 2, 2)] = total

    def masks_of(layer, mask):
        @pl.loop(0, 32)
        def _(e):
            m = mask[e].astype(F32)
            cnt[layer, e] = jnp.broadcast_to(jnp.sum(m, axis=0, keepdims=True), (8, 128))
            maskt[layer, e] = m.T.astype(BF)

    def slots_of(layer, sources):
        @pl.loop(0, 32)
        def _(i):
            who = peer(i)[1]

            def look(e, carry):
                seen, first, second = carry
                hit = owners[layer * 32 + e] == who
                first = jnp.where(jnp.logical_and(hit, seen == 0), e, first)
                second = jnp.where(jnp.logical_and(hit, seen == 1), e, second)
                return seen + hit.astype(jnp.int32), first, second

            zero = jnp.int32(0)
            seen, first, second = lax.fori_loop(0, 32, look, (zero, zero, zero), unroll=8)
            tab[layer, i, 0] = first
            tab[layer, i, 1] = second
            tab[layer, i, 2] = sources[first]
            tab[layer, i, 3] = sources[second]
            tab[layer, i, 4] = seen

    def meta_copy(i):
        return remote(msg_out.at[i], msg_in.at[i], meta_s.at[i], meta_r.at[i], peer(i))

    def message(i):
        row = lax.broadcasted_iota(jnp.int32, (8, 128), 0)
        msg = jnp.zeros((8, 128), F32)
        for layer, targets in ((0, tgt1), (1, tgt2)):
            for k in range(2):
                e = tab[layer, i, k]
                used = tab[layer, i, 4] > k
                place = jnp.where(used, targets[e] * 16, -1024).astype(F32)
                msg = jnp.where(row == layer * 4 + k, cnt[layer, e], msg)
                msg = jnp.where(row == layer * 4 + 2 + k, place, msg)
        return msg

    def meta_send():
        msg_in[0] = message(0)

        @pl.loop(1, 32)
        def _(i):
            msg_out[i] = message(i)
            meta_copy(i).start()

    def meta_wait():
        @pl.loop(1, 32)
        def _(i):
            meta_copy(i).wait()

    def build(layer):
        @pl.loop(0, 32)
        def _(i):
            msg = msg_in[i]
            for k in range(2):
                rows = pl.ds(pl.multiple_of(i * 32 + k * 16, 16), 16)
                place = msg[layer * 4 + 2 + k : layer * 4 + 3 + k, :]
                vcol[rows, :] = jnp.broadcast_to(place, (16, 128))
                count = msg[layer * 4 + k : layer * 4 + k + 1, :]
                ccol[rows, :] = jnp.broadcast_to(count, (16, 128)).astype(BF)

        ramp = lax.broadcasted_iota(jnp.int32, (1024, 128), 0) % 16
        vrow = (vcol[...] + ramp.astype(F32)).T[0:1, :]
        spot = lax.broadcasted_iota(jnp.int32, (256, 1024), 0).astype(F32)
        lhs[layer] = jnp.where(spot == vrow, 1.0, 0.0).astype(BF)
        degree = dot(lhs[layer], ccol[...])
        lane = lax.broadcasted_iota(jnp.int32, (256, 128), 1)
        within = lax.broadcasted_iota(jnp.int32, (256, 128), 0) % 16
        for g in range(8):
            here = jnp.sum(jnp.where(lane == within + g * 16, degree, 0.0), axis=1, keepdims=True)
            rdeg[g] = jnp.broadcast_to(1.0 / jnp.maximum(here, 1.0), (256, 128))

    def piece_copy(phase, i):
        c = phase % 2
        return remote(
            sendbuf[c].at[i], recv[phase].at[i], aa_s.at[phase, i], aa_r.at[phase, i], peer(i)
        )

    def piece(layer, values, c, i, k):
        return dot(maskt[layer, tab[layer, i, k]], values[c][tab[layer, i, 2 + k]]).astype(BF)

    def pieces(phase, values):
        layer, c = phase // 2, phase % 2
        if layer == 1:

            @pl.loop(1, 32)
            def _(i):
                piece_copy(c, i).wait_send()

        @pl.loop(1, 32)
        def _(i):
            for k in range(2):
                sendbuf[c][i, k] = piece(layer, values, c, i, k)
            piece_copy(phase, i).start()

        for k in range(2):
            recv[phase][0, k] = piece(layer, values, c, 0, k)

    def gather_tiles(phase, result):
        layer, c = phase // 2, phase % 2

        @pl.loop(1, 32)
        def _(i):
            piece_copy(phase, i).wait_recv()

        for g in range(8):
            rows = pl.ds(g * 16, 16)
            got = recv[phase][:, :, rows, :].reshape(1024, 128)
            mean = dot(lhs[layer], got) * rdeg[g]
            if layer == 0:
                mean = jnp.maximum(own[2 + c, :, rows, :].reshape(256, 128) + mean, 0.0)
            result[c][:, rows, :] = mean.astype(BF).reshape(16, 16, 128)

    far = (right, left, opp)

    def rows_copies(m, c, values):
        return [
            remote(
                values[c].at[pl.ds(d * 4, 4)], hm[m][c].at[f],
                rows_s.at[m, c, k], rows_r.at[m, c, k], (d, n),
            )
            for k, d in enumerate(far)
        ]

    def rows_send(m, c, values):
        start(rows_copies(m, c, values))
        hm[m][c][f] = values[c][pl.ds(f * 4, 4)]

    def rows_wait(m, c, values):
        for copy in rows_copies(m, c, values):
            copy.wait_recv()

    def cot_copies():
        return [
            remote(
                cot_hbm.at[pl.ds(pl.multiple_of(d * 512, 512), 512)], cot.at[f],
                cot_s.at[k], cot_r.at[k], (d, n),
            )
            for k, d in enumerate(far)
        ]

    chip = z * 4 + y
    slice_rows = pl.ds(pl.multiple_of(chip * 16, 16), 16)

    def w2_near(k):
        return remote(w2.at[core, f], w2.at[core, f], w2_s.at[k], w2_r.at[k], (far[k], n))

    def w2_first(m=0):
        src = (ws2_hbm, wn2_hbm)[m].at[slice_rows]
        return remote(src, wx, w2_s.at[2], w2_r.at[2], (opp, n))

    def w2_own():
        return local(wx, w2.at[core, opp, slice_rows], 10)

    def w2_spread(i):
        zz = (z + sign * (i // 4) + 4) % 4
        yy = (y + sign * (i % 4) + 4) % 4
        dev = (f, zz * 8 + yy * 2 + core)
        return remote(wx, w2.at[core, opp, slice_rows], ws_s.at[i], ws_r.at[i], dev)

    def w2_forward(d, k):
        return remote(
            w2.at[core, d], w2.at[core, d], wd_s.at[k], wd_r.at[k], (f, other)
        )

    def pre_add(m, c, first):
        left_side = jnp.concatenate([hm[m][c][s].reshape(512, 128) for s in range(4)], axis=1)

        @pl.loop(0, 4)
        def _(j):
            cols = pl.ds(pl.multiple_of(j * 256, 256), 256)
            part = dot(left_side, w2[m, :, c * 128 : (c + 1) * 128, cols].reshape(512, 256))
            for half in range(2):
                new = part[:, half * 128 : (half + 1) * 128].reshape(4, 128, 128)
                at = pl.ds(j * 4, 4)
                own[half, at] = new if first else own[half, at] + new

    def x_copy(c, m=0):
        return remote(hm[m][c], xoth[c], x_s.at[c], x_r.at[c], (f, other))

    def x_send(c):
        for m in range(2):

            @pl.when(core == 1 - m)
            def _():
                x_copy(c, m).start()

    def transpose_x(c):
        for m in range(2):

            @pl.when(core == m)
            def _():
                for s in range(4):
                    mine = hm[m][c][s].reshape(512, 128).astype(F32).T.astype(BF)
                    xt[c, s * 128 : (s + 1) * 128, 0:512] = mine

        x_copy(c).wait_recv()
        for s in range(4):
            theirs = xoth[c][s].reshape(512, 128).astype(F32).T.astype(BF)
            xt[c, s * 128 : (s + 1) * 128, 512:1024] = theirs

    def slope_copy():
        return remote(slope_own, slope_oth, sl_s.at[0], sl_r.at[0], (f, other))

    def h2_copies():
        return [
            remote(
                feat.at[pl.ds(pl.multiple_of(d * 512, 512), 512), pl.ds(0, 256)], hid2_out.at[pl.ds(pl.multiple_of(f * 512, 512), 512)],
                h2_s.at[k], h2_r.at[k], (d, n),
            )
            for k, d in enumerate(far)
        ]

    def along_y(d):
        return (f, z * 8 + ((y + d) % 4) * 2 + core)

    def along_z(d):
        return (f, ((z + d) % 4) * 8 + y * 2 + core)

    def g1_copies(h):
        out = []
        for d in (1, 2, 3):
            if h == 0:
                src, dev = g0.at[:, :, (y + d) % 4], along_y(d)
            else:
                src, dev = g1.at[:, (z + d) % 4], along_z(d)
            out.append(remote(src, r1[h].at[d - 1], g1_s.at[h, d - 1], g1_r.at[h, d - 1], dev))
        return out

    def g2_copies(h):
        out = []
        for d in (1, 2, 3):
            to = (z + d) % 4 if h == 0 else (y + d) % 4
            dev = along_z(d) if h == 0 else along_y(d)
            out.append(remote(s1[h].at[:, to], r2[h].at[d - 1], g2_s.at[h, d - 1], g2_r.at[h, d - 1], dev))
        return out

    def g3_copies(h):
        return [
            remote(
                s2[h].at[(f + d) % 4], r3[h].at[d - 1],
                g3_s.at[h, d - 1], g3_r.at[h, d - 1], ((f + d) % 4, n),
            )
            for d in (1, 2, 3)
        ]

    def fin_copy():
        rows = pl.ds(pl.multiple_of((1 - core) * 8, 8), 8)
        return remote(fin.at[rows], finr, fn_s.at[0], fn_r.at[0], (f, other))

    for m in range(2):

        @pl.when(core == m)
        def _():
            w2_first(m).start()

    loads[0].wait()
    loads[1].wait()
    project(NEIGH, opp, 0)
    start(copies_a(0))
    project(NEIGH, right, 1)
    project(NEIGH, left, 2)
    start(copies_direct(0))
    project(NEIGH, f, None)
    for c in loads[2:]:
        c.wait()
    w2_first().wait_recv()

    @pl.loop(1, 16)
    def _(i):
        w2_spread(i).start()

    w2_own().start()
    ring_add(0)
    start(copies_a(1))
    start(copies_direct(1))
    masks_of(0, mask1)
    slots_of(0, src1)
    project(SELF, opp, 0)
    ring_end(0)
    pieces(0, proj)
    ring_add(1)
    start(copies_a(2))
    project(SELF, right, 1)
    project(SELF, left, 2)
    start(copies_direct(2))
    project(SELF, f, None)
    load_mask2.wait()
    masks_of(1, mask2)
    slots_of(1, src2)
    meta_send()
    start(copies_a(3))
    ring_end(1)
    pieces(1, proj)
    ring_add(2)
    start(copies_direct(3))
    meta_wait()
    build(0)
    ring_add(3)

    for k in range(2):
        w2_near(k).start()
    ring_end(2)
    gather_tiles(0, hid)
    pieces(2, hid)
    rows_send(0, 0, hid)
    start(cot_copies())
    ring_end(3)
    gather_tiles(1, hid)
    pieces(3, hid)
    rows_send(0, 1, hid)
    w2_own().wait()

    @pl.loop(1, 16)
    def _(i):
        w2_spread(i).wait_recv()

    build(1)
    for k in range(2):
        w2_near(k).wait_recv()
    for k, d in enumerate(far):
        w2_forward(d, k).start()
    rows_wait(0, 0, hid)
    rows_wait(0, 1, hid)
    for k, d in enumerate(far):
        w2_forward(d, k).wait_recv()
    pre_add(0, 0, True)
    pre_add(0, 1, False)
    gather_tiles(2, proj)
    rows_send(1, 0, proj)
    rows_wait(1, 0, proj)
    x_send(0)
    pre_add(1, 0, False)
    transpose_x(0)
    gather_tiles(3, proj)
    rows_send(1, 1, proj)
    for c in cot_copies():
        c.wait_recv()
    rows_wait(1, 1, proj)
    x_send(1)
    pre_add(1, 1, False)
    for j in range(4):

        @pl.loop(0, 4)
        def _(t):
            rows = pl.ds(pl.multiple_of(t * 128, 128), 128)
            out_rows = pl.ds(pl.multiple_of(t * 128 + j * 512, 128), 128)
            for half in range(2):
                cols = slice(half * 128, (half + 1) * 128)
                v = own[half, j * 4 + t]
                s = 1.0 / (1.0 + jnp.exp(-v))
                feat[out_rows, cols] = (v * s).astype(BF)
                up = cot[j, rows, cols].astype(F32) * s * (1.0 + v * (1.0 - s))
                slope_own[j, rows, cols] = up.astype(BF)

    slope_copy().start()
    start(h2_copies())
    mine = pl.ds(pl.multiple_of(f * 512, 512), 512)
    hid2_out[mine, :] = feat[mine, 0:256]
    transpose_x(1)
    slope_copy().wait_recv()
    for j in range(4):
        up = jnp.concatenate([slope_own[j], slope_oth[j]], axis=0)
        grad = g0 if j < 2 else g1
        cols = pl.ds((j % 2) * 256, 256)
        for c in range(2):
            part = dot(xt[c], up).astype(BF)
            grad[:, 2 * c : 2 * c + 2, :, :, cols] = part.reshape(4, 2, 4, 16, 256)
        if j == 1:
            start(g1_copies(0))
        if j == 3:
            start(g1_copies(1))
    for h in range(2):
        for c in g1_copies(h):
            c.wait_recv()
        first = g0[:, :, y] if h == 0 else g1[:, z]
        total = first.astype(F32)
        for d in range(3):
            total = total + r1[h][d].astype(F32)
        s1[h][...] = total
        start(g2_copies(h))
    for h in range(2):
        for c in g2_copies(h):
            c.wait_recv()
        at = z if h == 0 else y
        s2[h][...] = s1[h][:, at] + r2[h][0] + r2[h][1] + r2[h][2]
        start(g3_copies(h))
    for h in range(2):
        for c in g3_copies(h):
            c.wait_recv()
        fin[:, h * 512 : (h + 1) * 512] = s2[h][f] + r3[h][0] + r3[h][1] + r3[h][2]
    fin_copy().start()
    fin_copy().wait_recv()
    mine8 = fin[pl.ds(pl.multiple_of(core * 8, 8), 8), :]
    first_core = jnp.full((8, 1024), core, jnp.int32) == 0
    gs_out[...] = jnp.where(first_core, mine8, finr[...])
    gn_out[...] = jnp.where(first_core, finr[...], mine8)

    for c in h2_copies():
        c.wait_recv()
    for q in range(4):
        for c in copies_a(q) + copies_direct(q) + copies_added(q):
            c.wait_send()

    @pl.loop(1, 16)
    def _(i):
        w2_spread(i).wait_send()

    @pl.loop(1, 32)
    def _(i):
        piece_copy(2, i).wait_send()
        piece_copy(3, i).wait_send()

    for m, values in ((0, hid), (1, proj)):
        for c in range(2):
            for copy in rows_copies(m, c, values):
                copy.wait_send()
    rest = cot_copies() + h2_copies() + [slope_copy(), fin_copy(), x_copy(0), x_copy(1)]
    rest += [w2_near(0), w2_near(1), w2_first()] + [w2_forward(d, k) for k, d in enumerate(far)]
    for h in range(2):
        rest += g1_copies(h) + g2_copies(h) + g3_copies(h)
    for copy in rest:
        copy.wait_send()


def local_step(
    features, self_w1, neigh_w1, self_w2, neigh_w2, source_tiles1, owner_blocks1, target_tiles1,
    tile_masks1, source_tiles2, owner_blocks2, target_tiles2, tile_masks2, cotangent,
):
    hbm = pl.BlockSpec(memory_space=pl.ANY)
    smem = pl.BlockSpec(memory_space=pltpu.SMEM)
    vmem = pl.BlockSpec(memory_space=pltpu.VMEM)
    v = pltpu.VMEM
    dma = pltpu.SemaphoreType.DMA

    def pair(*shape):
        return [dma(shape), dma(shape)]

    i32 = jnp.int32
    scratch = [
        v((2048, 512), BF), *[v((512, 1024), BF)] * 2, *[v((32, 128, 128), i32)] * 2,
        v((2, 32, 128, 128), BF), v((2, 32, 8, 128), F32), pltpu.SMEM((2, 32, 8), i32),
        *[v((3, 2048, 128), BF)] * 4, v((4, 16, 128, 128), F32), *[v((2, 1024, 128), BF)] * 4,
        *[v((2, 2048, 128), BF)] * 4, *[v((16, 128, 128), BF)] * 4,
        v((32, 8, 128), F32), v((32, 8, 128), F32), v((1024, 128), F32), v((1024, 128), BF),
        v((2, 256, 1024), BF), v((8, 256, 128), F32),
        *[v((32, 2, 128, 128), BF)] * 6, *[v((4, 4, 128, 128), BF)] * 6, v((2, 512, 1024), BF),
        v((4, 512, 256), BF), v((2, 4, 256, 1024), BF), v((16, 1024), BF), *[v((4, 512, 256), BF)] * 2,
        *[v((4, 4, 4, 16, 512), BF)] * 2, *[v((3, 4, 4, 16, 512), BF)] * 2,
        *[v((4, 4, 16, 512), F32)] * 2, *[v((3, 4, 16, 512), F32)] * 2, *[v((4, 16, 512), F32)] * 2,
        *[v((3, 16, 512), F32)] * 2, v((16, 1024), F32), v((8, 1024), F32),
        dma((11,)),
        *pair(32), *pair(4, 2), *pair(4, 4), *pair(4, 32), *pair(2, 2, 3), *pair(3), *pair(3),
        *pair(16), *pair(3), *pair(2), *pair(1), *pair(3), *pair(2, 3), *pair(2, 3), *pair(2, 3), *pair(1),
    ]
    hidden2, grad_self, grad_neigh = pl.pallas_call(
        kernel,
        out_shape=(
            jax.ShapeDtypeStruct((2048, 256), BF),
            jax.ShapeDtypeStruct((8, 1024), F32),
            jax.ShapeDtypeStruct((8, 1024), F32),
        ),
        in_specs=[hbm] * 5 + [smem] * 2 + [hbm] + [smem] * 2 + [hbm, smem, hbm],
        out_specs=(vmem, vmem, vmem),
        scratch_shapes=scratch,
        compiler_params=pltpu.CompilerParams(
            collective_id=0, has_side_effects=True, vmem_limit_bytes=(64 << 20) - (64 << 10)
        ),
        cost_estimate=pl.CostEstimate(flops=10**10, bytes_accessed=16 << 20, transcendentals=1 << 19),
        name="sage",
    )(
        features, self_w1, neigh_w1, self_w2, neigh_w2, source_tiles1, target_tiles1, tile_masks1,
        source_tiles2, target_tiles2, tile_masks2,
        jnp.concatenate([owner_blocks1[:, 0], owner_blocks2[:, 0]]), cotangent,
    )
    return hidden2, grad_self, grad_neigh


def solution(mesh):
    node3 = P("node", None, None)
    in_specs = (
        P("node", "feat"), P("feat", None), P("feat", None), P("feat", None), P("feat", None),
        P("node"), P("node", None), P("node"), node3,
        P("node"), P("node", None), P("node"), node3, P("node", "feat"),
    )
    out_specs = (P("node", "feat"), P(("feat", "node"), None), P(("feat", "node"), None))
    return jax.shard_map(local_step, mesh=mesh, in_specs=in_specs, out_specs=out_specs, check_vma=False)
```

```python
import functools

import jax
import jax.numpy as jnp
from jax import lax
from jax.experimental import pallas as pl
from jax.experimental.pallas import tpu as pltpu
from jax.sharding import PartitionSpec as P

MESH = pl.DeviceIdType.MESH
BF = jnp.bfloat16
F32 = jnp.float32
NEIGH, SELF = 0, 1


def dot(a, b):
    return jnp.dot(a, b, preferred_element_type=F32)


def kernel(
    feat_hbm, ws1_hbm, wn1_hbm, ws2_hbm, wn2_hbm,
    src1, tgt1, mask1_hbm, src2, tgt2, mask2_hbm, owners, cot_hbm,
    hid2_out, gs_out, gn_out,
    feat, w1n, w1s, mask1, mask2, maskt, cnt, tab,
    p0, p1, p2, p3, own, a0, a1, a2, a3, b0, b1, b2, b3, proj0, proj1, hid0, hid1,
    msg_out, msg_in, vcol, ccol, lhs, rdeg,
    send0, send1, recv0, recv1, recv2, recv3, h0, h1, m0, m1, xoth0, xoth1, xt,
    cot, w2, wx, u0, u1, u2, u3, o0, o1, o2, o3,
    g0, g1, r1a, r1b, s1a, s1b, r2a, r2b, s2a, s2b, r3a, r3b, fin, finr,
    ld, meta_s, meta_r, ra_s, ra_r, rb_s, rb_r, aa_s, aa_r, rows_s, rows_r,
    cot_s, cot_r, w2_s, w2_r, ws_s, ws_r, wd_s, wd_r, x_s, x_r, sl_s, sl_r, h2_s, h2_r,
    g1_s, g1_r, g2_s, g2_r, g3_s, g3_r, fn_s, fn_r,
):
    f = lax.axis_index("feat")
    n = lax.axis_index("node")
    z, y, core = n // 8, (n // 2) % 4, n % 2
    sign = 1 - 2 * core
    right, left, opp = (f + 1) % 4, (f + 3) % 4, (f + 2) % 4
    other = n + sign
    proj, hid = (proj0, proj1), (hid0, hid1)
    psend, buf_a, buf_b = (p0, p1, p2, p3), (a0, a1, a2, a3), (b0, b1, b2, b3)
    sendbuf, recv = (send0, send1), (recv0, recv1, recv2, recv3)
    hm, xoth = ((h0, h1), (m0, m1)), (xoth0, xoth1)
    slope_own, slope_oth = (u0, u1, u2, u3), (o0, o1, o2, o3)
    r1, s1, r2, s2, r3 = (r1a, r1b), (s1a, s1b), (r2a, r2b), (s2a, s2b), (r3a, r3b)

    def peer(i):
        j, ii, dc = i // 8, (i // 2) % 4, i % 2
        zz = (z + sign * ii + 4) % 4
        yy = (y + sign * ((ii + j) % 4) + 4) % 4
        return (f, zz * 8 + yy * 2 + (core + dc) % 2)

    def remote(src, dst, ss, rs, dev):
        return pltpu.make_async_remote_copy(
            src_ref=src, dst_ref=dst, send_sem=ss, recv_sem=rs, device_id=dev, device_id_type=MESH
        )

    def local(src, dst, k):
        return pltpu.make_async_copy(src, dst, ld.at[k])

    loads = [
        local(feat_hbm, feat, 0),
        local(wn1_hbm, w1n, 1),
        local(ws1_hbm, w1s, 2),
        local(mask1_hbm, mask1, 3),
        local(cot_hbm.at[pl.ds(pl.multiple_of(f * 512, 512), 512)], cot.at[f], 4),
    ]
    for m, ref in ((0, ws2_hbm), (1, wn2_hbm)):
        loads.append(local(ref, w2.at[m, f], 5 + m))
    load_mask2 = local(mask2_hbm, mask2, 9)
    for c in [*loads, load_mask2]:
        c.start()

    barrier = pltpu.get_barrier_semaphore()

    @pl.loop(1, 32)
    def _(i):
        pl.semaphore_signal(barrier, inc=1, device_id=peer(i), device_id_type=MESH)

    for d in (right, left, opp):
        pl.semaphore_signal(barrier, inc=1, device_id=(d, n), device_id_type=MESH)
    pl.semaphore_wait(barrier, 34)

    def project(mat, j, where):
        cols = pl.ds(pl.multiple_of(j * 256, 256), 256)

        @pl.loop(0, 4)
        def _(t):
            rows = pl.ds(pl.multiple_of(t * 512, 512), 512)
            part = dot(feat[rows, :], (w1n, w1s)[mat][:, cols])
            for c in range(2):
                half = part[:, c * 128 : (c + 1) * 128]
                if where is None:
                    own[2 * mat + c, pl.ds(t * 4, 4)] = half.reshape(4, 128, 128)
                else:
                    psend[2 * mat + c][where, rows, :] = half.astype(BF)

    lo, hi = pl.ds(0, 1024), pl.ds(1024, 1024)

    def copies_a(q):
        return [
            remote(psend[q].at[0, lo], buf_a[q].at[0], ra_s.at[q, 0], ra_r.at[q, 0], (right, n)),
            remote(psend[q].at[0, hi], buf_a[q].at[1], ra_s.at[q, 1], ra_r.at[q, 1], (left, n)),
        ]

    def copies_direct(q):
        return [
            remote(psend[q].at[1, hi], buf_b[q].at[0, hi], rb_s.at[q, 0], rb_r.at[q, 0], (right, n)),
            remote(psend[q].at[2, lo], buf_b[q].at[1, lo], rb_s.at[q, 1], rb_r.at[q, 1], (left, n)),
        ]

    def copies_added(q):
        return [
            remote(psend[q].at[1, lo], buf_b[q].at[0, lo], rb_s.at[q, 2], rb_r.at[q, 2], (right, n)),
            remote(psend[q].at[2, hi], buf_b[q].at[1, hi], rb_s.at[q, 3], rb_r.at[q, 3], (left, n)),
        ]

    def start(copies):
        for c in copies:
            c.start()

    def ring_add(q):
        a, b = copies_a(q), copies_added(q)
        for s, base in ((0, 0), (1, 1024)):
            a[s].wait_recv()

            @pl.loop(0, 4)
            def _(t):
                rows = pl.ds(pl.multiple_of(t * 256 + base, 256), 256)
                from_rows = pl.ds(pl.multiple_of(t * 256, 256), 256)
                total = psend[q][1 + s, rows, :].astype(F32) + buf_a[q][s, from_rows, :].astype(F32)
                psend[q][1 + s, rows, :] = total.astype(BF)

            b[s].start()

    def ring_end(q):
        for c in copies_direct(q) + copies_added(q):
            c.wait_recv()

        @pl.loop(0, 8)
        def _(t):
            rows = pl.ds(pl.multiple_of(t * 256, 256), 256)
            got = buf_b[q][0, rows, :].astype(F32) + buf_b[q][1, rows, :].astype(F32)
            total = own[q, pl.ds(t * 2, 2)] + got.reshape(2, 128, 128)
            if q < 2:
                proj[q][pl.ds(t * 2, 2)] = total.astype(BF)
            else:
                own[q, pl.ds(t * 2, 2)] = total

    def masks_of(layer, mask):
        @pl.loop(0, 32)
        def _(e):
            m = mask[e].astype(F32)
            cnt[layer, e] = jnp.broadcast_to(jnp.sum(m, axis=0, keepdims=True), (8, 128))
            maskt[layer, e] = m.T.astype(BF)

    def slots_of(layer, sources):
        @pl.loop(0, 32)
        def _(i):
            who = peer(i)[1]

            def look(e, carry):
                seen, first, second = carry
                hit = owners[layer * 32 + e] == who
                first = jnp.where(jnp.logical_and(hit, seen == 0), e, first)
                second = jnp.where(jnp.logical_and(hit, seen == 1), e, second)
                return seen + hit.astype(jnp.int32), first, second

            zero = jnp.int32(0)
            seen, first, second = lax.fori_loop(0, 32, look, (zero, zero, zero), unroll=8)
            tab[layer, i, 0] = first
            tab[layer, i, 1] = second
            tab[layer, i, 2] = sources[first]
            tab[layer, i, 3] = sources[second]
            tab[layer, i, 4] = seen

    def meta_copy(i):
        return remote(msg_out.at[i], msg_in.at[i], meta_s.at[i], meta_r.at[i], peer(i))

    def message(i):
        row = lax.broadcasted_iota(jnp.int32, (8, 128), 0)
        msg = jnp.zeros((8, 128), F32)
        for layer, targets in ((0, tgt1), (1, tgt2)):
            for k in range(2):
                e = tab[layer, i, k]
                used = tab[layer, i, 4] > k
                place = jnp.where(used, targets[e] * 16, -1024).astype(F32)
                msg = jnp.where(row == layer * 4 + k, cnt[layer, e], msg)
                msg = jnp.where(row == layer * 4 + 2 + k, place, msg)
        return msg

    def meta_send():
        msg_in[0] = message(0)

        @pl.loop(1, 32)
        def _(i):
            msg_out[i] = message(i)
            meta_copy(i).start()

    def meta_wait():
        @pl.loop(1, 32)
        def _(i):
            meta_copy(i).wait()

    def build(layer):
        @pl.loop(0, 32)
        def _(i):
            msg = msg_in[i]
            for k in range(2):
                rows = pl.ds(pl.multiple_of(i * 32 + k * 16, 16), 16)
                place = msg[layer * 4 + 2 + k : layer * 4 + 3 + k, :]
                vcol[rows, :] = jnp.broadcast_to(place, (16, 128))
                count = msg[layer * 4 + k : layer * 4 + k + 1, :]
                ccol[rows, :] = jnp.broadcast_to(count, (16, 128)).astype(BF)

        ramp = lax.broadcasted_iota(jnp.int32, (1024, 128), 0) % 16
        vrow = (vcol[...] + ramp.astype(F32)).T[0:1, :]
        spot = lax.broadcasted_iota(jnp.int32, (256, 1024), 0).astype(F32)
        lhs[layer] = jnp.where(spot == vrow, 1.0, 0.0).astype(BF)
        degree = dot(lhs[layer], ccol[...])
        lane = lax.broadcasted_iota(jnp.int32, (256, 128), 1)
        within = lax.broadcasted_iota(jnp.int32, (256, 128), 0) % 16
        for g in range(8):
            here = jnp.sum(jnp.where(lane == within + g * 16, degree, 0.0), axis=1, keepdims=True)
            rdeg[g] = jnp.broadcast_to(1.0 / jnp.maximum(here, 1.0), (256, 128))

    def piece_copy(phase, i):
        c = phase % 2
        return remote(
            sendbuf[c].at[i], recv[phase].at[i], aa_s.at[phase, i], aa_r.at[phase, i], peer(i)
        )

    def piece(layer, values, c, i, k):
        return dot(maskt[layer, tab[layer, i, k]], values[c][tab[layer, i, 2 + k]]).astype(BF)

    def pieces(phase, values):
        layer, c = phase // 2, phase % 2
        if layer == 1:

            @pl.loop(1, 32)
            def _(i):
                piece_copy(c, i).wait_send()

        @pl.loop(1, 32)
        def _(i):
            for k in range(2):
                sendbuf[c][i, k] = piece(layer, values, c, i, k)
            piece_copy(phase, i).start()

        for k in range(2):
            recv[phase][0, k] = piece(layer, values, c, 0, k)

    def gather_tiles(phase, result):
        layer, c = phase // 2, phase % 2

        @pl.loop(1, 32)
        def _(i):
            piece_copy(phase, i).wait_recv()

        for g in range(8):
            rows = pl.ds(g * 16, 16)
            got = recv[phase][:, :, rows, :].reshape(1024, 128)
            mean = dot(lhs[layer], got) * rdeg[g]
            if layer == 0:
                mean = jnp.maximum(own[2 + c, :, rows, :].reshape(256, 128) + mean, 0.0)
            result[c][:, rows, :] = mean.astype(BF).reshape(16, 16, 128)

    far = (right, left, opp)

    def rows_copies(m, c, values):
        return [
            remote(
                values[c].at[pl.ds(d * 4, 4)], hm[m][c].at[f],
                rows_s.at[m, c, k], rows_r.at[m, c, k], (d, n),
            )
            for k, d in enumerate(far)
        ]

    def rows_send(m, c, values):
        start(rows_copies(m, c, values))
        hm[m][c][f] = values[c][pl.ds(f * 4, 4)]

    def rows_wait(m, c, values):
        for copy in rows_copies(m, c, values):
            copy.wait_recv()

    def cot_copies():
        return [
            remote(
                cot_hbm.at[pl.ds(pl.multiple_of(d * 512, 512), 512)], cot.at[f],
                cot_s.at[k], cot_r.at[k], (d, n),
            )
            for k, d in enumerate(far)
        ]

    chip = z * 4 + y
    slice_rows = pl.ds(pl.multiple_of(chip * 16, 16), 16)

    def w2_near(k):
        return remote(w2.at[core, f], w2.at[core, f], w2_s.at[k], w2_r.at[k], (far[k], n))

    def w2_first(m=0):
        src = (ws2_hbm, wn2_hbm)[m].at[slice_rows]
        return remote(src, wx, w2_s.at[2], w2_r.at[2], (opp, n))

    def w2_own():
        return local(wx, w2.at[core, opp, slice_rows], 10)

    def w2_spread(i):
        zz = (z + sign * (i // 4) + 4) % 4
        yy = (y + sign * (i % 4) + 4) % 4
        dev = (f, zz * 8 + yy * 2 + core)
        return remote(wx, w2.at[core, opp, slice_rows], ws_s.at[i], ws_r.at[i], dev)

    def w2_forward(d, k):
        return remote(
            w2.at[core, d], w2.at[core, d], wd_s.at[k], wd_r.at[k], (f, other)
        )

    def pre_add(m, c, first):
        left_side = jnp.concatenate([hm[m][c][s].reshape(512, 128) for s in range(4)], axis=1)

        @pl.loop(0, 4)
        def _(j):
            cols = pl.ds(pl.multiple_of(j * 256, 256), 256)
            part = dot(left_side, w2[m, :, c * 128 : (c + 1) * 128, cols].reshape(512, 256))
            for half in range(2):
                new = part[:, half * 128 : (half + 1) * 128].reshape(4, 128, 128)
                at = pl.ds(j * 4, 4)
                own[half, at] = new if first else own[half, at] + new

    def x_copy(c, m=0):
        return remote(hm[m][c], xoth[c], x_s.at[c], x_r.at[c], (f, other))

    def x_send(c):
        for m in range(2):

            @pl.when(core == 1 - m)
            def _():
                x_copy(c, m).start()

    def transpose_x(c):
        for m in range(2):

            @pl.when(core == m)
            def _():
                for s in range(4):
                    mine = hm[m][c][s].reshape(512, 128).astype(F32).T.astype(BF)
                    xt[c, s * 128 : (s + 1) * 128, 0:512] = mine

        x_copy(c).wait_recv()
        for s in range(4):
            theirs = xoth[c][s].reshape(512, 128).astype(F32).T.astype(BF)
            xt[c, s * 128 : (s + 1) * 128, 512:1024] = theirs

    def slope_copy(j):
        return remote(slope_own[j], slope_oth[j], sl_s.at[j], sl_r.at[j], (f, other))

    def h2_copies():
        return [
            remote(
                feat.at[pl.ds(pl.multiple_of(d * 512, 512), 512), pl.ds(0, 256)], hid2_out.at[pl.ds(pl.multiple_of(f * 512, 512), 512)],
                h2_s.at[k], h2_r.at[k], (d, n),
            )
            for k, d in enumerate(far)
        ]

    def along_y(d):
        return (f, z * 8 + ((y + d) % 4) * 2 + core)

    def along_z(d):
        return (f, ((z + d) % 4) * 8 + y * 2 + core)

    def g1_copies(h):
        out = []
        for d in (1, 2, 3):
            if h == 0:
                src, dev = g0.at[:, :, (y + d) % 4], along_y(d)
            else:
                src, dev = g1.at[:, (z + d) % 4], along_z(d)
            out.append(remote(src, r1[h].at[d - 1], g1_s.at[h, d - 1], g1_r.at[h, d - 1], dev))
        return out

    def g2_copies(h):
        out = []
        for d in (1, 2, 3):
            to = (z + d) % 4 if h == 0 else (y + d) % 4
            dev = along_z(d) if h == 0 else along_y(d)
            out.append(remote(s1[h].at[:, to], r2[h].at[d - 1], g2_s.at[h, d - 1], g2_r.at[h, d - 1], dev))
        return out

    def g3_copies(h):
        return [
            remote(
                s2[h].at[(f + d) % 4], r3[h].at[d - 1],
                g3_s.at[h, d - 1], g3_r.at[h, d - 1], ((f + d) % 4, n),
            )
            for d in (1, 2, 3)
        ]

    def fin_copy():
        rows = pl.ds(pl.multiple_of((1 - core) * 8, 8), 8)
        return remote(fin.at[rows], finr, fn_s.at[0], fn_r.at[0], (f, other))

    for m in range(2):

        @pl.when(core == m)
        def _():
            w2_first(m).start()

    loads[0].wait()
    loads[1].wait()
    project(NEIGH, opp, 0)
    start(copies_a(0))
    project(NEIGH, right, 1)
    project(NEIGH, left, 2)
    start(copies_direct(0))
    project(NEIGH, f, None)
    for c in loads[2:]:
        c.wait()
    w2_first().wait_recv()

    @pl.loop(1, 16)
    def _(i):
        w2_spread(i).start()

    w2_own().start()
    ring_add(0)
    start(copies_a(1))
    start(copies_direct(1))
    masks_of(0, mask1)
    slots_of(0, src1)
    project(SELF, opp, 0)
    ring_end(0)
    pieces(0, proj)
    ring_add(1)
    start(copies_a(2))
    project(SELF, right, 1)
    project(SELF, left, 2)
    start(copies_direct(2))
    project(SELF, f, None)
    load_mask2.wait()
    masks_of(1, mask2)
    slots_of(1, src2)
    meta_send()
    start(copies_a(3))
    ring_end(1)
    pieces(1, proj)
    ring_add(2)
    start(copies_direct(3))
    meta_wait()
    build(0)
    ring_add(3)

    for k in range(2):
        w2_near(k).start()
    ring_end(2)
    gather_tiles(0, hid)
    pieces(2, hid)
    rows_send(0, 0, hid)
    start(cot_copies())
    ring_end(3)
    gather_tiles(1, hid)
    pieces(3, hid)
    rows_send(0, 1, hid)
    w2_own().wait()

    @pl.loop(1, 16)
    def _(i):
        w2_spread(i).wait_recv()

    build(1)
    for k in range(2):
        w2_near(k).wait_recv()
    for k, d in enumerate(far):
        w2_forward(d, k).start()
    rows_wait(0, 0, hid)
    rows_wait(0, 1, hid)
    for k, d in enumerate(far):
        w2_forward(d, k).wait_recv()
    pre_add(0, 0, True)
    pre_add(0, 1, False)
    gather_tiles(2, proj)
    rows_send(1, 0, proj)
    rows_wait(1, 0, proj)
    x_send(0)
    pre_add(1, 0, False)
    transpose_x(0)
    gather_tiles(3, proj)
    rows_send(1, 1, proj)
    for c in cot_copies():
        c.wait_recv()
    rows_wait(1, 1, proj)
    x_send(1)
    pre_add(1, 1, False)
    for j in range(4):

        @pl.loop(0, 4)
        def _(t):
            rows = pl.ds(pl.multiple_of(t * 128, 128), 128)
            out_rows = pl.ds(pl.multiple_of(t * 128 + j * 512, 128), 128)
            for half in range(2):
                cols = slice(half * 128, (half + 1) * 128)
                v = own[half, j * 4 + t]
                s = 1.0 / (1.0 + jnp.exp(-v))
                feat[out_rows, cols] = (v * s).astype(BF)
                up = cot[j, rows, cols].astype(F32) * s * (1.0 + v * (1.0 - s))
                slope_own[j][rows, cols] = up.astype(BF)

        slope_copy(j).start()

    start(h2_copies())
    mine = pl.ds(pl.multiple_of(f * 512, 512), 512)
    hid2_out[mine, :] = feat[mine, 0:256]
    transpose_x(1)
    for j in range(4):
        slope_copy(j).wait_recv()
        up = jnp.concatenate([slope_own[j][...], slope_oth[j][...]], axis=0)
        grad = g0 if j < 2 else g1
        cols = pl.ds((j % 2) * 256, 256)
        for c in range(2):
            part = dot(xt[c], up).astype(BF)
            grad[:, 2 * c : 2 * c + 2, :, :, cols] = part.reshape(4, 2, 4, 16, 256)
        if j == 1:
            start(g1_copies(0))
        if j == 3:
            start(g1_copies(1))
    for h in range(2):
        for c in g1_copies(h):
            c.wait_recv()
        first = g0[:, :, y] if h == 0 else g1[:, z]
        total = first.astype(F32)
        for d in range(3):
            total = total + r1[h][d].astype(F32)
        s1[h][...] = total
        start(g2_copies(h))
    for h in range(2):
        for c in g2_copies(h):
            c.wait_recv()
        at = z if h == 0 else y
        s2[h][...] = s1[h][:, at] + r2[h][0] + r2[h][1] + r2[h][2]
        start(g3_copies(h))
    for h in range(2):
        for c in g3_copies(h):
            c.wait_recv()
        fin[:, h * 512 : (h + 1) * 512] = s2[h][f] + r3[h][0] + r3[h][1] + r3[h][2]
    fin_copy().start()
    fin_copy().wait_recv()
    mine8 = fin[pl.ds(pl.multiple_of(core * 8, 8), 8), :]
    first_core = jnp.full((8, 1024), core, jnp.int32) == 0
    gs_out[...] = jnp.where(first_core, mine8, finr[...])
    gn_out[...] = jnp.where(first_core, finr[...], mine8)

    for c in h2_copies():
        c.wait_recv()
    for q in range(4):
        for c in copies_a(q) + copies_direct(q) + copies_added(q):
            c.wait_send()

    @pl.loop(1, 16)
    def _(i):
        w2_spread(i).wait_send()

    @pl.loop(1, 32)
    def _(i):
        piece_copy(2, i).wait_send()
        piece_copy(3, i).wait_send()

    for m, values in ((0, hid), (1, proj)):
        for c in range(2):
            for copy in rows_copies(m, c, values):
                copy.wait_send()
    rest = cot_copies() + h2_copies() + [fin_copy(), x_copy(0), x_copy(1)] + [slope_copy(j) for j in range(4)]
    rest += [w2_near(0), w2_near(1), w2_first()] + [w2_forward(d, k) for k, d in enumerate(far)]
    for h in range(2):
        rest += g1_copies(h) + g2_copies(h) + g3_copies(h)
    for copy in rest:
        copy.wait_send()


def local_step(
    features, self_w1, neigh_w1, self_w2, neigh_w2, source_tiles1, owner_blocks1, target_tiles1,
    tile_masks1, source_tiles2, owner_blocks2, target_tiles2, tile_masks2, cotangent,
):
    hbm = pl.BlockSpec(memory_space=pl.ANY)
    smem = pl.BlockSpec(memory_space=pltpu.SMEM)
    vmem = pl.BlockSpec(memory_space=pltpu.VMEM)
    v = pltpu.VMEM
    dma = pltpu.SemaphoreType.DMA

    def pair(*shape):
        return [dma(shape), dma(shape)]

    i32 = jnp.int32
    scratch = [
        v((2048, 512), BF), *[v((512, 1024), BF)] * 2, *[v((32, 128, 128), i32)] * 2,
        v((2, 32, 128, 128), BF), v((2, 32, 8, 128), F32), pltpu.SMEM((2, 32, 8), i32),
        *[v((3, 2048, 128), BF)] * 4, v((4, 16, 128, 128), F32), *[v((2, 1024, 128), BF)] * 4,
        *[v((2, 2048, 128), BF)] * 4, *[v((16, 128, 128), BF)] * 4,
        v((32, 8, 128), F32), v((32, 8, 128), F32), v((1024, 128), F32), v((1024, 128), BF),
        v((2, 256, 1024), BF), v((8, 256, 128), F32),
        *[v((32, 2, 128, 128), BF)] * 6, *[v((4, 4, 128, 128), BF)] * 6, v((2, 512, 1024), BF),
        v((4, 512, 256), BF), v((2, 4, 256, 1024), BF), v((16, 1024), BF), *[v((512, 256), BF)] * 8,
        *[v((4, 4, 4, 16, 512), BF)] * 2, *[v((3, 4, 4, 16, 512), BF)] * 2,
        *[v((4, 4, 16, 512), F32)] * 2, *[v((3, 4, 16, 512), F32)] * 2, *[v((4, 16, 512), F32)] * 2,
        *[v((3, 16, 512), F32)] * 2, v((16, 1024), F32), v((8, 1024), F32),
        dma((11,)),
        *pair(32), *pair(4, 2), *pair(4, 4), *pair(4, 32), *pair(2, 2, 3), *pair(3), *pair(3),
        *pair(16), *pair(3), *pair(2), *pair(4), *pair(3), *pair(2, 3), *pair(2, 3), *pair(2, 3), *pair(1),
    ]
    hidden2, grad_self, grad_neigh = pl.pallas_call(
        kernel,
        out_shape=(
            jax.ShapeDtypeStruct((2048, 256), BF),
            jax.ShapeDtypeStruct((8, 1024), F32),
            jax.ShapeDtypeStruct((8, 1024), F32),
        ),
        in_specs=[hbm] * 5 + [smem] * 2 + [hbm] + [smem] * 2 + [hbm, smem, hbm],
        out_specs=(vmem, vmem, vmem),
        scratch_shapes=scratch,
        compiler_params=pltpu.CompilerParams(
            collective_id=0, has_side_effects=True, vmem_limit_bytes=(64 << 20) - (64 << 10)
        ),
        cost_estimate=pl.CostEstimate(flops=10**10, bytes_accessed=16 << 20, transcendentals=1 << 19),
        name="sage",
    )(
        features, self_w1, neigh_w1, self_w2, neigh_w2, source_tiles1, target_tiles1, tile_masks1,
        source_tiles2, target_tiles2, tile_masks2,
        jnp.concatenate([owner_blocks1[:, 0], owner_blocks2[:, 0]]), cotangent,
    )
    return hidden2, grad_self, grad_neigh


def solution(mesh):
    node3 = P("node", None, None)
    in_specs = (
        P("node", "feat"), P("feat", None), P("feat", None), P("feat", None), P("feat", None),
        P("node"), P("node", None), P("node"), node3,
        P("node"), P("node", None), P("node"), node3, P("node", "feat"),
    )
    out_specs = (P("node", "feat"), P(("feat", "node"), None), P(("feat", "node"), None))
    return jax.shard_map(local_step, mesh=mesh, in_specs=in_specs, out_specs=out_specs, check_vma=False)
```
